32 devices in a mesh: lon: 8 (over z, core), lat: 2 (over y), dp: 2 (over x).
Axes of the slice: x: 2, y: 2, z: 4, core: 2. Of those that a mesh axis runs over, the one named last changes fastest.
Arguments:
- states: bfloat16 [2, 32, 512, 192], P('dp', 'lat', 'lon'), may hold values from -6 to 6
- cotangent: bfloat16 [2, 32, 512, 192], P('dp', 'lat', 'lon'), may hold values from -6 to 6
- kernel: bfloat16 [3, 3, 192, 192], replicated, may hold values from -0.15625 to 0.15625
- land_mask: int32 [32, 512], P('lat', 'lon'), may hold values 0 or 1
- ocean_tiles: int32 [2, 8, 3], P('lat', 'lon'), may hold values from 0 to 4, as said below
Outputs:
- output: bfloat16 [2, 32, 512, 192], P('dp', 'lat', 'lon')
- state_grad: bfloat16 [2, 32, 512, 192], P('dp', 'lat', 'lon')
- weight_grad: float32 [3, 3, 192, 192], replicated
The draws below stay inside these ranges and needn't reach their ends.
Inputs may be any that keep to these rules, and one draw needn't show every extreme that they name: `ocean_tiles`: each device's 3 entries are distinct tile numbers of its block in increasing order, followed by the value 4 in unused slots; at least one slot is used, and some device uses all of them.
All inputs are finite; a program needn't handle non-finite values. No bound on the sum of `land_mask` on one device may be relied on, other than what follows from the above.
Results may differ from the reference program's by a relative error of at most 0.0049.
Values may be sent and summed in bfloat16 or wider, within the bound.
A program may use at most 64 MiB of HBM per device.

```python
import math
import jax
import jax.numpy as jnp
from jax import lax

C = 192
TS = 16
CY = 16
CX = 64
BATCH = 2
NY = 32
NX = 512
TPD = 4
CAP = 3
N_LON = 8
N_LAT = 2


def draw_ocean_tiles(key, part):
    key = jax.random.fold_in(key, 17)
    devices_all = N_LAT * N_LON
    score_key, count_key, pick_key = jax.random.split(key, 3)
    score_table = jax.random.randint(score_key, (devices_all, TPD), 0, 1 << 30)
    tile_order = jnp.argsort(score_table, axis=1, stable=True).astype(jnp.int32)
    chosen = jnp.sort(tile_order[:, :CAP], axis=1)
    lowest = max(CAP // 2, 1)
    live_count = jax.random.randint(count_key, (devices_all,), lowest, CAP + 1)
    fullest = jax.random.randint(pick_key, (), 0, devices_all)
    device_ids = jnp.arange(devices_all)
    live_count = jnp.where(device_ids == fullest, CAP, live_count)
    live_count = jnp.where(device_ids == (fullest + 1) % devices_all, lowest, live_count)
    slot_index = jnp.arange(CAP)[None, :]
    listed = jnp.where(slot_index < live_count[:, None], chosen, TPD)
    return listed.reshape(N_LAT, N_LON, CAP).astype(jnp.int32)


def touch_ends(values, own_key, smallest, largest):
    index_at = [jax.random.randint(jax.random.fold_in(own_key, axis), (), 0, length) for axis, length in enumerate(values.shape)]
    widest = values.shape.index(max(values.shape))
    beside = index_at[:widest] + [(index_at[widest] + 1) % values.shape[widest]] + index_at[widest + 1:]
    return values.at[tuple(index_at)].set(smallest).at[tuple(beside)].set(largest)


def steps_of(key, shape, cuts, smallest, high):
    def one(axis_at, parts):
        steps = jax.random.uniform(jax.random.fold_in(jax.random.fold_in(key, 6), axis_at), (parts,), jnp.float32, smallest / len(cuts), high / len(cuts))
        return jnp.repeat(jnp.exp(steps), shape[axis_at] // parts).reshape((-1,) + (1,) * (len(shape) - axis_at - 1))

    level = one(*cuts[0])
    for cut in cuts[1:]:
        level = level * one(*cut)
    return level


def scatter_about(rng, extent, width, most, cuts=(), kind=jnp.bfloat16):
    result = jax.random.normal(rng, extent, jnp.float32) * width
    if len(cuts) > 0:
        result = steps_of(rng, extent, cuts, -0.22, 0.18) * result
    return jnp.clip(result, min=-most, max=most).astype(kind)


def setup_inputs(seed: int = 0) -> dict:
    key_list = jax.random.split(jax.random.key(seed), 6)
    return {
        "states": scatter_about(key_list[0], (BATCH, NY, NX, C), 1.0, 6.0, ((0, 2), (1, 2), (2, 8))),
        "cotangent": scatter_about(key_list[1], (BATCH, NY, NX, C), 1.0, 6.0, ((0, 2), (1, 2), (2, 8))),
        "kernel": scatter_about(key_list[2], (3, 3, C, C), (9 * C) ** -0.5, 0.15625),
        "land_mask": touch_ends((jax.random.randint(key_list[3], (NY, NX), 0, 4) < 3).astype(jnp.int32), jax.random.fold_in(key_list[3], 1), 0, 1),
        "ocean_tiles": draw_ocean_tiles(jax.random.fold_in(key_list[5], 71), 0),
    }


def live_cells(ocean_tiles):
    tile_rows = CY // TS
    tile_cols = CX // TS
    numbers = jnp.arange(TPD, dtype=jnp.int32)
    hit = jnp.any(ocean_tiles[..., None] == numbers, axis=2)
    table = hit.reshape(N_LAT, N_LON, tile_rows, tile_cols).transpose(0, 2, 1, 3)
    table = table.reshape(N_LAT * tile_rows, N_LON * tile_cols).astype(jnp.float32)
    return jnp.repeat(jnp.repeat(table, TS, axis=0), TS, axis=1)

def pad_fold(masked):
    wrapped = jnp.concatenate([masked[:, :, -1:], masked, masked[:, :, :1]], axis=2)
    north = jnp.flip(wrapped[:, -1:], axis=2)
    return jnp.concatenate([jnp.zeros_like(north), wrapped, north], axis=1)

def reference(states, cotangent, kernel, land_mask, ocean_tiles):
    keep_cells = land_mask.astype(jnp.float32) * live_cells(ocean_tiles)
    keep_full = keep_cells[None, :, :, None]
    masked = jnp.where(keep_full > 0, states, jnp.zeros_like(states))
    padded = pad_fold(masked)
    channels = states.shape[3]
    flat_count = BATCH * NY * NX
    preact = jnp.zeros((BATCH, NY, NX, channels), jnp.float32)
    for row_shift in range(3):
        for col_shift in range(3):
            window = padded[:, row_shift:row_shift + NY, col_shift:col_shift + NX].reshape(flat_count, channels)
            term = jnp.dot(window, kernel[row_shift, col_shift], preferred_element_type=jnp.float32)
            preact = preact + term.reshape(BATCH, NY, NX, channels)
    sigmoid_h = jax.nn.sigmoid(preact)
    output = (keep_full * preact * sigmoid_h).astype(jnp.bfloat16)
    slope = sigmoid_h * (1.0 + preact * (1.0 - sigmoid_h))
    grad_pre = (keep_full * cotangent.astype(jnp.float32) * slope).astype(jnp.bfloat16)
    grad_flat = grad_pre.reshape(flat_count, channels)
    grad_pad = jnp.zeros((BATCH, NY + 2, NX + 2, channels), jnp.float32)
    kernel_terms = []
    for row_shift in range(3):
        for col_shift in range(3):
            window = padded[:, row_shift:row_shift + NY, col_shift:col_shift + NX].reshape(flat_count, channels)
            kernel_terms.append(lax.dot_general(window, grad_flat, (((0,), (0,)), ((), ())), preferred_element_type=jnp.float32))
            backed = jnp.dot(grad_flat, kernel[row_shift, col_shift].T, preferred_element_type=jnp.float32)
            grad_pad = grad_pad.at[:, row_shift:row_shift + NY, col_shift:col_shift + NX].add(backed.reshape(BATCH, NY, NX, channels))
    weight_grad = jnp.stack(kernel_terms).reshape(3, 3, channels, channels) / math.sqrt(flat_count)
    unfolded = grad_pad[:, 1:NY + 1]
    unfolded = unfolded.at[:, NY - 1].add(jnp.flip(grad_pad[:, NY + 1], axis=1))
    inner = unfolded[:, :, 1:NX + 1]
    inner = inner.at[:, :, NX - 1].add(unfolded[:, :, 0])
    inner = inner.at[:, :, 0].add(unfolded[:, :, NX + 1])
    state_grad = (keep_full * inner).astype(jnp.bfloat16)
    return (output, state_grad, weight_grad)
```

```python
import functools
import math

import jax
import jax.numpy as jnp
from jax import lax
from jax.experimental import pallas as pl
from jax.experimental.pallas import tpu as pltpu
from jax.sharding import PartitionSpec as P

TS = 16
LANE = 128
SUB = 16
MESH = pl.DeviceIdType.MESH
F32 = jnp.float32
BF16 = jnp.bfloat16
NORTH, SOUTH = 0, 1


def iota(shape, axis):
    return lax.broadcasted_iota(jnp.int32, shape, axis)


def mm(a, b, dims=((1,), (0,))):
    return lax.dot_general(a, b, (dims, ((), ())), preferred_element_type=F32)


def onehot(cond):
    return jnp.where(cond, 1.0, 0.0).astype(BF16)


def kernel_body(
    geo,
    states, cotangent, weights, land, tiles,
    out, sgrad, wgrad,
    own, colsend, colrecv, halo, wide_x, wide_g, lag_g, k_fwd, k_bwd, k_north,
    wf, wb, r1, a1, b1, r2, a2, b2, r3, ag,
    hs_send, hs_recv, s1, q1, s2, q2, s3, q3, s4, q4, s5, q5, s6, q6,
):
    n_lon, n_lat, n_dp, scale = geo
    _, rows, cols, ch = states.shape
    cells = rows * cols
    wide = 2 * LANE
    lon, lat, dp = lax.axis_index("lon"), lax.axis_index("lat"), lax.axis_index("dp")
    core, z = lax.rem(lon, 2), lon // 2
    nz, npl = n_lon // 2, n_lat * n_dp
    plane = lat * n_dp + dp
    left = {"lon": lax.rem(lon + n_lon - 1, n_lon)}
    right = {"lon": lax.rem(lon + 1, n_lon)}
    top = lat == n_lat - 1
    mirror = {"lon": n_lon - 1 - lon}
    upward = {
        "lon": jnp.where(top, n_lon - 1 - lon, lon),
        "lat": jnp.where(top, lat, lat + 1),
    }
    up_slot = jnp.where(top, NORTH, SOUTH)
    downward = {"lat": jnp.maximum(lat - 1, 0)}
    pair = {"lon": lon + 1 - 2 * core}

    def plane_peer(d):
        index = lax.rem(plane + d, npl)
        return index, {"lat": index // n_dp, "dp": lax.rem(index, n_dp)}

    def z_peer(d):
        index = lax.rem(z + d, nz)
        return index, {"lon": index * 2 + core}

    def remote(src, dst, send, recv, where):
        return pltpu.make_async_remote_copy(
            src_ref=src, dst_ref=dst, send_sem=send, recv_sem=recv,
            device_id=where, device_id_type=MESH,
        )

    barrier = pltpu.get_barrier_semaphore()

    def greet(where):
        pl.semaphore_signal(barrier, inc=1, device_id=where, device_id_type=MESH)

    greet(left)
    greet(right)
    for d in range(1, npl):
        greet(plane_peer(d)[1])
    for d in range(1, nz):
        greet(z_peer(d)[1])

    @pl.when(top)
    def _():
        greet(mirror)

    tile_cols = cols // TS
    number = iota((rows, cols), 0) // TS * tile_cols + iota((rows, cols), 1) // TS
    hit = number == tiles[0, 0, 0]
    for slot in range(1, tiles.shape[2]):
        hit = hit | (number == tiles[0, 0, slot])
    keep_plane = jnp.where(hit, land[...], 0).astype(F32).astype(BF16)
    cell = iota((cells, rows), 0) - cols * iota((cells, rows), 1)
    by_row = mm(onehot((cell >= 0) & (cell < cols)), keep_plane)
    pos = lax.rem(iota((cells, cols), 0), cols)
    by_cell = jnp.where(pos == iota((cells, cols), 1), by_row, 0.0).astype(BF16)
    keep = mm(by_cell, jnp.ones((cols, ch), BF16))
    column = lax.rem(iota((cells, ch), 0), cols)
    at_first, at_last = column == 0, column == cols - 1
    first_of = onehot(cell == 0)
    last_of = onehot(cell == cols - 1)
    pick = iota((2 * rows, cells), 1) - jnp.where(
        iota((2 * rows, cells), 0) < rows,
        cols * iota((2 * rows, cells), 0),
        cols * (iota((2 * rows, cells), 0) - rows) + cols - 1,
    )
    pick = onehot(pick == 0)

    masked = jnp.where(keep > 0, states[...].reshape(cells, ch).astype(F32), 0.0)
    own[0] = masked.astype(BF16)
    colsend[0] = mm(pick, own[0]).astype(BF16)

    k_fwd[...] = jnp.zeros_like(k_fwd)
    k_bwd[...] = jnp.zeros_like(k_bwd)
    k_north[...] = jnp.zeros_like(k_north)
    wide_x[...] = jnp.zeros_like(wide_x)
    wide_g[...] = jnp.zeros_like(wide_g)
    lag_g[...] = jnp.zeros_like(lag_g)
    for r in range(3):
        for c in range(3):
            k_fwd[r, c * wide : c * wide + ch, :] = weights[r, c]
            k_bwd[r, :, c * wide : c * wide + ch] = weights[r, c]

    @pl.when(top)
    def _():
        for c in range(3):
            k_north[:, c * wide : c * wide + ch] = weights[2, 2 - c]

    @pl.when(jnp.logical_not(top))
    def _():
        for c in range(3):
            k_north[:, c * wide : c * wide + ch] = weights[0, c]

    @pl.when(lat == 0)
    def _():
        for which in range(2):
            halo[which, SOUTH] = jnp.zeros_like(halo[which, SOUTH])

    pl.semaphore_wait(barrier, 2 + (npl - 1) + (nz - 1) + jnp.where(top, 1, 0))

    def first_copies(w):
        send, recv = hs_send.at[w], hs_recv.at[w]
        to_left = remote(
            colsend.at[w, pl.ds(0, rows)], colrecv.at[w, pl.ds(rows, rows)],
            send.at[0], recv.at[0], left)
        to_right = remote(
            colsend.at[w, pl.ds(rows, rows)], colrecv.at[w, pl.ds(0, rows)],
            send.at[1], recv.at[1], right)
        up = remote(
            own.at[w, pl.ds(cells - cols, cols)], halo.at[w, up_slot, pl.ds(0, cols)],
            send.at[2], recv.at[2 + up_slot], upward)
        down = remote(
            own.at[w, pl.ds(0, cols)], halo.at[w, NORTH, pl.ds(0, cols)],
            send.at[3], recv.at[2 + NORTH], downward)
        return to_left, to_right, up, down

    def corner_copies(w):
        send, recv = hs_send.at[w], hs_recv.at[w]
        up = remote(
            colrecv.at[w], halo.at[w, up_slot, pl.ds(cols, 2 * rows)],
            send.at[4], recv.at[4 + up_slot], upward)
        down = remote(
            colrecv.at[w], halo.at[w, NORTH, pl.ds(cols, 2 * rows)],
            send.at[5], recv.at[4 + NORTH], downward)
        return up, down

    def start_first(w):
        to_left, to_right, up, down = first_copies(w)
        to_left.start()
        to_right.start()
        up.start()

        @pl.when(lat > 0)
        def _():
            down.start()

    def pass_corners(w):
        to_left, to_right, _, _ = first_copies(w)
        to_left.wait_recv()
        to_right.wait_recv()
        up, down = corner_copies(w)
        up.start()

        @pl.when(lat > 0)
        def _():
            down.start()

    def finish_halo(w):
        send, recv = hs_send.at[w], hs_recv.at[w]

        def arrived(slot):
            remote(own.at[w, pl.ds(0, cols)], halo.at[w, slot, pl.ds(0, cols)],
                   send.at[3], recv.at[2 + slot], downward).wait_recv()
            remote(colrecv.at[w], halo.at[w, slot, pl.ds(cols, 2 * rows)],
                   send.at[5], recv.at[4 + slot], downward).wait_recv()

        arrived(NORTH)

        @pl.when(lat > 0)
        def _():
            arrived(SOUTH)

    def finish_sends(w):
        to_left, to_right, up, down = first_copies(w)
        up2, down2 = corner_copies(w)
        for copy in (to_left, to_right, up, up2):
            copy.wait_send()

        @pl.when(lat > 0)
        def _():
            down.wait_send()
            down2.wait_send()

    def spread(w, ref, values, order):
        lane = [b * wide for b in order]
        body = pl.ds(cols, cells)
        ref[body, lane[1] : lane[1] + ch] = own[w]
        low = mm(first_of, colrecv[w, :rows])
        ref[body, lane[0] : lane[0] + ch] = jnp.where(
            at_first, low, pltpu.roll(values, 1, 0)
        ).astype(BF16)
        high = mm(last_of, colrecv[w, rows:])
        ref[body, lane[2] : lane[2] + ch] = jnp.where(
            at_last, high, pltpu.roll(values, cells - 1, 0)
        ).astype(BF16)

    def spread_halo(w, ref, order):
        shape = (3 * cols, cols + 2 * rows)
        p, s = iota(shape, 0), iota(shape, 1)
        block = jnp.where(p >= cols, 1, 0) + jnp.where(p >= 2 * cols, 1, 0)
        east = p - cols * block + block - 1
        flip = jnp.where(top, 1, 0)
        for slot, at in ((NORTH, cells + cols), (SOUTH, 0)):
            if slot == NORTH:
                e = east + flip * (cols - 1 - 2 * east)
                edge = flip * (rows - 1)
            else:
                e, edge = east, rows - 1
            source = jnp.where(
                e < 0, cols + edge, jnp.where(e >= cols, cols + rows + edge, e))
            got = mm(onehot(s == source), halo[w, slot]).astype(BF16)
            for b in range(3):
                ref[at : at + cols, order[b] * wide : order[b] * wide + ch] = got[
                    b * cols : (b + 1) * cols
                ]

    start_first(0)
    pass_corners(0)
    spread(0, wide_x, masked, (0, 1, 2))
    finish_halo(0)
    spread_halo(0, wide_x, (0, 1, 2))

    pre = mm(wide_x[0:cells, :], k_fwd[0])
    pre = pre + mm(wide_x[cols : cols + cells, :], k_fwd[1])
    pre = pre + mm(wide_x[2 * cols : 2 * cols + cells, :], k_fwd[2])
    sig = 1.0 / (1.0 + jnp.exp(-pre))
    out[...] = (keep * pre * sig).astype(BF16).reshape(out.shape)
    slope = sig * (1.0 + pre * (1.0 - sig))
    grad = (keep * cotangent[...].reshape(cells, ch).astype(F32) * slope).astype(BF16)
    own[1] = grad
    for r in range(3):
        lag_g[r * cols : r * cols + cells, r * wide : r * wide + ch] = grad
    colsend[1] = mm(pick, own[1]).astype(BF16)
    start_first(1)

    full = mm(wide_x[...], lag_g[...], ((0,), (0,)))
    units = ch // SUB
    total = wf.shape[0]

    def put(slab, value):
        value = value.reshape(units, SUB, LANE)
        wf[slab * units : (slab + 1) * units] = value
        wb[slab * units : (slab + 1) * units] = value.astype(BF16)

    tails = []
    for c in range(3):
        band = full[c * wide : c * wide + ch]
        for r in range(3):
            put(3 * c + r, band[:, r * wide : r * wide + LANE])
        rest = [band[:, r * wide + LANE : (r + 1) * wide] for r in range(3)]
        put(9 + c, rest[0] + pltpu.roll(rest[1], LANE // 2, 1))
        tails.append(rest[2])
    put(12, tails[0] + pltpu.roll(tails[1], LANE // 2, 1))
    put(13, tails[2])
    if total > 14 * units:
        wf[14 * units :] = jnp.zeros_like(wf[14 * units :])
        wb[14 * units :] = jnp.zeros_like(wb[14 * units :])

    half = total // 2
    per = half // npl
    chunk = -(-per // nz)
    pair_copy = remote(
        wb.at[pl.ds((1 - core) * half, half)], r1, s1.at[0], q1.at[0], pair)
    pair_copy.start()
    pass_corners(1)
    spread(1, wide_g, grad.astype(F32), (2, 1, 0))
    pair_copy.wait()
    first = wf[pl.ds(core * half, half)] + r1[...].astype(F32)
    a1[...] = first.reshape(a1.shape)
    b1[...] = first.reshape(a1.shape).astype(BF16)
    plane_copies = []
    for d in range(1, npl):
        index, where = plane_peer(d)
        copy = remote(b1.at[index], r2.at[d - 1], s2.at[d - 1], q2.at[d - 1], where)
        copy.start()
        plane_copies.append(copy)

    finish_halo(1)
    spread_halo(1, wide_g, (2, 1, 0))
    nt = ((1,), (1,))
    back = mm(wide_g[cols : cols + cells, :], k_bwd[1], nt)
    back = back + mm(wide_g[0:cells, :], k_bwd[2], nt)
    inner = mm(wide_g[2 * cols : cols + cells, :], k_bwd[0], nt)
    edge = mm(wide_g[cols + cells : 2 * cols + cells, :], k_north[...], nt)
    back = back + jnp.concatenate([inner, edge], axis=0)
    sgrad[...] = jnp.where(keep > 0, back, 0.0).astype(BF16).reshape(sgrad.shape)

    for copy in plane_copies:
        copy.wait()
    second = a1[plane]
    for d in range(npl - 1):
        second = second + r2[d].astype(F32)
    a2[0:per] = second
    b2[0:per] = second.astype(BF16)
    if nz * chunk > per:
        a2[per:] = jnp.zeros_like(a2[per:])
        b2[per:] = jnp.zeros_like(b2[per:])
    z_copies = []
    for d in range(1, nz):
        index, where = z_peer(d)
        copy = remote(
            b2.at[pl.ds(index * chunk, chunk)], r3.at[d - 1],
            s3.at[d - 1], q3.at[d - 1], where)
        copy.start()
        z_copies.append(copy)
    for copy in z_copies:
        copy.wait()
    third = a2[pl.ds(z * chunk, chunk)]
    for d in range(nz - 1):
        third = third + r3[d].astype(F32)
    mine = pl.ds(z * chunk, chunk)
    ag[core, plane, mine] = (third * scale).astype(BF16)

    z_back = []
    for d in range(1, nz):
        _, where = z_peer(d)
        here = ag.at[core, plane, mine]
        copy = remote(here, here, s4.at[d - 1], q4.at[d - 1], where)
        copy.start()
        z_back.append(copy)
    for d in range(1, nz):
        source = lax.rem(z + nz - d, nz)
        there = ag.at[core, plane, pl.ds(source * chunk, chunk)]
        remote(there, there, s4.at[d - 1], q4.at[d - 1], pair).wait_recv()
    whole = pl.ds(0, per)
    here = ag.at[core, plane, whole]
    plane_back = []
    for d in range(1, npl):
        _, where = plane_peer(d)
        copy = remote(here, here, s5.at[d - 1], q5.at[d - 1], where)
        copy.start()
        plane_back.append(copy)
    core_back = [remote(here, here, s6.at[0], q6.at[0], pair)]
    core_back[0].start()
    for d in range(1, npl):
        source = lax.rem(plane + npl - d, npl)
        there = ag.at[core, source, whole]
        remote(there, there, s5.at[d - 1], q5.at[d - 1], pair).wait_recv()
        copy = remote(there, there, s6.at[d], q6.at[d], pair)
        copy.start()
        core_back.append(copy)
    for d in range(npl):
        source = lax.rem(plane + npl - d, npl)
        there = ag.at[1 - core, source, whole]
        remote(there, there, s6.at[d], q6.at[d], pair).wait_recv()

    def slab(s):
        found = []
        for t in range(s * units, (s + 1) * units):
            found.append(ag[t // half, t % half // per, t % per])
        return jnp.concatenate(found, axis=0).astype(F32)

    hl = LANE // 2
    for c in range(3):
        for r in range(3):
            wgrad[r, c, :, 0:LANE] = slab(3 * c + r)
        rest = slab(9 + c)
        wgrad[0, c, :, LANE:ch] = rest[:, 0:hl]
        wgrad[1, c, :, LANE:ch] = pltpu.roll(rest, hl, 1)[:, 0:hl]
    rest = slab(12)
    wgrad[2, 0, :, LANE:ch] = rest[:, 0:hl]
    wgrad[2, 1, :, LANE:ch] = pltpu.roll(rest, hl, 1)[:, 0:hl]
    wgrad[2, 2, :, LANE:ch] = slab(13)[:, 0:hl]

    finish_sends(0)
    finish_sends(1)
    for copy in z_back + plane_back + core_back:
        copy.wait_send()


def body(states, cotangent, weights, land_mask, ocean_tiles):
    n_lon, n_lat, n_dp = (lax.axis_size(a) for a in ("lon", "lat", "dp"))
    batch, rows, cols, ch = states.shape
    assert batch == 1 and ch == 192 and n_lon % 2 == 0
    cells = rows * cols
    count = batch * n_dp * rows * n_lat * cols * n_lon
    wide = 2 * LANE
    nz, npl = n_lon // 2, n_lat * n_dp
    groups = 2 * npl
    total = -(-14 * (ch // SUB) // groups) * groups
    half = total // 2
    per = half // npl
    chunk = -(-per // nz)
    tile = (SUB, LANE)
    vmem = pltpu.VMEM
    dma = pltpu.SemaphoreType.DMA
    scratch = [
        vmem((2, cells, ch), BF16),
        vmem((2, 2 * rows, ch), BF16),
        vmem((2, 2 * rows, ch), BF16),
        vmem((2, 2, cols + 2 * rows, ch), BF16),
        vmem((cells + 2 * cols, 3 * wide), BF16),
        vmem((cells + 2 * cols, 3 * wide), BF16),
        vmem((cells + 2 * cols, 3 * wide), BF16),
        vmem((3, 3 * wide, ch), BF16),
        vmem((3, ch, 3 * wide), BF16),
        vmem((ch, 3 * wide), BF16),
        vmem((total,) + tile, F32),
        vmem((total,) + tile, BF16),
        vmem((half,) + tile, BF16),
        vmem((npl, per) + tile, F32),
        vmem((npl, per) + tile, BF16),
        vmem((npl - 1, per) + tile, BF16),
        vmem((nz * chunk,) + tile, F32),
        vmem((nz * chunk,) + tile, BF16),
        vmem((nz - 1, chunk) + tile, BF16),
        vmem((2, npl, nz * chunk) + tile, BF16),
        dma((2, 6)), dma((2, 6)),
        dma((1,)), dma((1,)),
        dma((npl - 1,)), dma((npl - 1,)),
        dma((nz - 1,)), dma((nz - 1,)),
        dma((nz - 1,)), dma((nz - 1,)),
        dma((npl - 1,)), dma((npl - 1,)),
        dma((npl,)), dma((npl,)),
    ]
    in_vmem = pl.BlockSpec(memory_space=pltpu.VMEM)
    geo = (n_lon, n_lat, n_dp, 1.0 / math.sqrt(count))
    return pl.pallas_call(
        functools.partial(kernel_body, geo),
        out_shape=(
            jax.ShapeDtypeStruct(states.shape, BF16),
            jax.ShapeDtypeStruct(states.shape, BF16),
            jax.ShapeDtypeStruct(weights.shape, F32),
        ),
        in_specs=[in_vmem] * 4 + [pl.BlockSpec(memory_space=pltpu.SMEM)],
        out_specs=(in_vmem,) * 3,
        scratch_shapes=scratch,
        compiler_params=pltpu.CompilerParams(
            collective_id=0, has_side_effects=True, vmem_limit_bytes=48 * 2**20
        ),
        cost_estimate=pl.CostEstimate(
            flops=54 * cells * ch * ch, bytes_accessed=5_000_000, transcendentals=cells * ch
        ),
    )(states, cotangent, weights, land_mask, ocean_tiles)


def solution(mesh):
    in_specs = (
        P("dp", "lat", "lon", None),
        P("dp", "lat", "lon", None),
        P(),
        P("lat", "lon"),
        P("lat", "lon", None),
    )
    out_specs = (P("dp", "lat", "lon", None), P("dp", "lat", "lon", None), P())
    return jax.shard_map(body, mesh=mesh, in_specs=in_specs, out_specs=out_specs, check_vma=False)
```

```python
import functools
import math

import jax
import jax.numpy as jnp
from jax import lax
from jax.experimental import pallas as pl
from jax.experimental.pallas import tpu as pltpu
from jax.sharding import PartitionSpec as P

TS = 16
LANE = 128
SUB = 16
MESH = pl.DeviceIdType.MESH
F32 = jnp.float32
BF16 = jnp.bfloat16
NORTH, SOUTH = 0, 1


def iota(shape, axis):
    return lax.broadcasted_iota(jnp.int32, shape, axis)


def mm(a, b, dims=((1,), (0,))):
    return lax.dot_general(a, b, (dims, ((), ())), preferred_element_type=F32)


def onehot(cond):
    return jnp.where(cond, 1.0, 0.0).astype(BF16)


def kernel_body(
    geo,
    states_hbm, cotangent_hbm, weights_hbm, land_hbm, tiles,
    out_hbm, sgrad_hbm, wgrad_hbm,
    out, sgrad, wgrad, states, cotangent, weights, land, in_sem, out_sem,
    own, colsend, colrecv, halo, wide_x, wide_g, lag_g, k_fwd, k_bwd, k_north,
    x_turned, parts, hs_send, hs_recv,
):
    n_lon, n_lat, n_dp, scale = geo
    _, rows, cols, ch = states.shape
    cells = rows * cols
    wide = 2 * LANE
    lon, lat, dp = lax.axis_index("lon"), lax.axis_index("lat"), lax.axis_index("dp")
    core, z = lax.rem(lon, 2), lon // 2
    nz, npl = n_lon // 2, n_lat * n_dp
    plane = lat * n_dp + dp
    left = {"lon": lax.rem(lon + n_lon - 1, n_lon)}
    right = {"lon": lax.rem(lon + 1, n_lon)}
    top = lat == n_lat - 1
    mirror = {"lon": n_lon - 1 - lon}
    upward = {
        "lon": jnp.where(top, n_lon - 1 - lon, lon),
        "lat": jnp.where(top, lat, lat + 1),
    }
    up_slot = jnp.where(top, NORTH, SOUTH)
    downward = {"lat": jnp.maximum(lat - 1, 0)}
    pair = {"lon": lon + 1 - 2 * core}

    def plane_peer(d):
        index = lax.rem(plane + d, npl)
        return index, {"lat": index // n_dp, "dp": lax.rem(index, n_dp)}

    def z_peer(d):
        index = lax.rem(z + d, nz)
        return index, {"lon": index * 2 + core}

    def remote(src, dst, send, recv, where):
        return pltpu.make_async_remote_copy(
            src_ref=src, dst_ref=dst, send_sem=send, recv_sem=recv,
            device_id=where, device_id_type=MESH,
        )

    fetch = []
    for i, (src, dst) in enumerate((
        (land_hbm, land), (states_hbm, states), (weights_hbm, weights),
        (cotangent_hbm, cotangent),
    )):
        copy = pltpu.make_async_copy(src, dst, in_sem.at[i])
        copy.start()
        fetch.append(copy)
    stores = []

    def store(src, dst):
        copy = pltpu.make_async_copy(src, dst, out_sem.at[len(stores)])
        copy.start()
        stores.append(copy)

    barrier = pltpu.get_barrier_semaphore()

    def greet(where):
        pl.semaphore_signal(barrier, inc=1, device_id=where, device_id_type=MESH)

    greet(left)
    greet(right)
    for d in range(1, npl):
        greet(plane_peer(d)[1])
    for d in range(1, nz):
        greet(z_peer(d)[1])

    @pl.when(top)
    def _():
        greet(mirror)

    tile_cols = cols // TS
    number = iota((rows, cols), 0) // TS * tile_cols + iota((rows, cols), 1) // TS
    hit = number == tiles[0, 0, 0]
    for slot in range(1, tiles.shape[2]):
        hit = hit | (number == tiles[0, 0, slot])
    fetch[0].wait()
    keep_plane = jnp.where(hit, land[...], 0).astype(F32).astype(BF16)
    cell = iota((cells, rows), 0) - cols * iota((cells, rows), 1)
    by_row = mm(onehot((cell >= 0) & (cell < cols)), keep_plane)
    pos = iota((cells, cols), 0) & (cols - 1)
    by_cell = jnp.where(pos == iota((cells, cols), 1), by_row, 0.0).astype(BF16)
    keep = mm(by_cell, jnp.ones((cols, ch), BF16))
    column = iota((cells, ch), 0) & (cols - 1)
    at_first, at_last = column == 0, column == cols - 1
    first_of = onehot(cell == 0)
    last_of = onehot(cell == cols - 1)
    pick = iota((2 * rows, cells), 1) - jnp.where(
        iota((2 * rows, cells), 0) < rows,
        cols * iota((2 * rows, cells), 0),
        cols * (iota((2 * rows, cells), 0) - rows) + cols - 1,
    )
    pick = onehot(pick == 0)

    fetch[1].wait()
    masked = jnp.where(keep > 0, states[...].reshape(cells, ch).astype(F32), 0.0)
    own[0] = masked.astype(BF16)
    colsend[0] = mm(pick, own[0]).astype(BF16)

    @pl.when(lat == 0)
    def _():
        for which in range(2):
            halo[which, SOUTH] = jnp.zeros_like(halo[which, SOUTH])

    pl.semaphore_wait(barrier, 2 + (npl - 1) + (nz - 1) + jnp.where(top, 1, 0))

    def first_copies(w):
        send, recv = hs_send.at[w], hs_recv.at[w]
        to_left = remote(
            colsend.at[w, pl.ds(0, rows)], colrecv.at[w, pl.ds(rows, rows)],
            send.at[0], recv.at[0], left)
        to_right = remote(
            colsend.at[w, pl.ds(rows, rows)], colrecv.at[w, pl.ds(0, rows)],
            send.at[1], recv.at[1], right)
        up = remote(
            own.at[w, pl.ds(cells - cols, cols)], halo.at[w, up_slot, pl.ds(0, cols)],
            send.at[2], recv.at[2 + up_slot], upward)
        down = remote(
            own.at[w, pl.ds(0, cols)], halo.at[w, NORTH, pl.ds(0, cols)],
            send.at[3], recv.at[2 + NORTH], downward)
        return to_left, to_right, up, down

    def corner_copies(w):
        send, recv = hs_send.at[w], hs_recv.at[w]
        up = remote(
            colrecv.at[w], halo.at[w, up_slot, pl.ds(cols, 2 * rows)],
            send.at[4], recv.at[4 + up_slot], upward)
        down = remote(
            colrecv.at[w], halo.at[w, NORTH, pl.ds(cols, 2 * rows)],
            send.at[5], recv.at[4 + NORTH], downward)
        return up, down

    def start_first(w):
        to_left, to_right, up, down = first_copies(w)
        to_left.start()
        to_right.start()
        up.start()

        @pl.when(lat > 0)
        def _():
            down.start()

    def pass_corners(w):
        to_left, to_right, _, _ = first_copies(w)
        to_left.wait_recv()
        to_right.wait_recv()
        up, down = corner_copies(w)
        up.start()

        @pl.when(lat > 0)
        def _():
            down.start()

    def finish_halo(w):
        send, recv = hs_send.at[w], hs_recv.at[w]

        def arrived(slot):
            remote(own.at[w, pl.ds(0, cols)], halo.at[w, slot, pl.ds(0, cols)],
                   send.at[3], recv.at[2 + slot], downward).wait_recv()
            remote(colrecv.at[w], halo.at[w, slot, pl.ds(cols, 2 * rows)],
                   send.at[5], recv.at[4 + slot], downward).wait_recv()

        arrived(NORTH)

        @pl.when(lat > 0)
        def _():
            arrived(SOUTH)

    def finish_sends(w):
        to_left, to_right, up, down = first_copies(w)
        up2, down2 = corner_copies(w)
        for copy in (to_left, to_right, up, up2):
            copy.wait_send()

        @pl.when(lat > 0)
        def _():
            down.wait_send()
            down2.wait_send()

    def spread(w, ref, values, order):
        lane = [b * wide for b in order]
        body = pl.ds(cols, cells)
        ref[body, lane[1] : lane[1] + ch] = own[w]
        low = mm(first_of, colrecv[w, :rows])
        ref[body, lane[0] : lane[0] + ch] = jnp.where(
            at_first, low, pltpu.roll(values, 1, 0)
        ).astype(BF16)
        high = mm(last_of, colrecv[w, rows:])
        ref[body, lane[2] : lane[2] + ch] = jnp.where(
            at_last, high, pltpu.roll(values, cells - 1, 0)
        ).astype(BF16)

    def spread_halo(w, ref, order):
        shape = (3 * cols, cols + 2 * rows)
        p, s = iota(shape, 0), iota(shape, 1)
        block = jnp.where(p >= cols, 1, 0) + jnp.where(p >= 2 * cols, 1, 0)
        east = p - cols * block + block - 1
        flip = jnp.where(top, 1, 0)
        for slot, at in ((NORTH, cells + cols), (SOUTH, 0)):
            if slot == NORTH:
                e = east + flip * (cols - 1 - 2 * east)
                edge = flip * (rows - 1)
            else:
                e, edge = east, rows - 1
            source = jnp.where(
                e < 0, cols + edge, jnp.where(e >= cols, cols + rows + edge, e))
            got = mm(onehot(s == source), halo[w, slot]).astype(BF16)
            for b in range(3):
                ref[at : at + cols, order[b] * wide : order[b] * wide + ch] = got[
                    b * cols : (b + 1) * cols
                ]

    start_first(0)
    fetch[2].wait()
    k_north[...] = jnp.zeros_like(k_north)
    for c in range(3):
        gap = pl.ds(c * wide + LANE, LANE)
        for ref in (wide_x, wide_g, lag_g):
            ref[:, gap] = jnp.zeros((ref.shape[0], LANE), BF16)
        for lo, hi in ((0, c * cols), (c * cols + cells, cells + 2 * cols)):
            if hi > lo:
                lag_g[lo:hi, c * wide : (c + 1) * wide] = jnp.zeros((hi - lo, wide), BF16)
    for r in range(3):
        k_bwd[r] = jnp.zeros_like(k_bwd[r])
        k_fwd[r] = jnp.zeros_like(k_fwd[r])
    for r in range(3):
        for c in range(3):
            k_fwd[r, c * wide : c * wide + ch, :] = weights[r, c]
            k_bwd[r, :, c * wide : c * wide + ch] = weights[r, c]

    @pl.when(top)
    def _():
        for c in range(3):
            k_north[:, c * wide : c * wide + ch] = weights[2, 2 - c]

    @pl.when(jnp.logical_not(top))
    def _():
        for c in range(3):
            k_north[:, c * wide : c * wide + ch] = weights[0, c]

    pass_corners(0)
    spread(0, wide_x, masked, (0, 1, 2))
    pre = mm(wide_x[cols : cols + cells, :], k_fwd[1])
    low = mm(wide_x[cols:cells, :], k_fwd[0])
    high = mm(wide_x[2 * cols : cols + cells, :], k_fwd[2])
    finish_halo(0)
    spread_halo(0, wide_x, (0, 1, 2))
    low_edge = mm(wide_x[0:cols, :], k_fwd[0])
    high_edge = mm(wide_x[cells + cols :, :], k_fwd[2])
    pre = pre + jnp.concatenate([low_edge, low], axis=0)
    pre = pre + jnp.concatenate([high, high_edge], axis=0)
    fetch[3].wait()
    for c in range(3):
        x_turned[c] = wide_x[:, c * wide : (c + 1) * wide].T
    sig = 1.0 / (1.0 + jnp.exp(-pre))
    out[...] = (keep * pre * sig).astype(BF16).reshape(out.shape)
    store(out, out_hbm)
    slope = sig * (1.0 + pre * (1.0 - sig))
    grad = (keep * cotangent[...].reshape(cells, ch).astype(F32) * slope).astype(BF16)
    own[1] = grad
    for r in range(3):
        lag_g[r * cols : r * cols + cells, r * wide : r * wide + ch] = grad
    colsend[1] = mm(pick, own[1]).astype(BF16)
    start_first(1)

    units = ch // SUB
    hl = LANE // 2
    tails = {}

    def add_up(p):
        q = parts[p]
        full = mm(x_turned[p], lag_g[...])
        band = full[:ch]
        slabs = [band[:, r * wide : r * wide + LANE] for r in range(3)]
        rest = [band[:, r * wide + LANE : (r + 1) * wide] for r in range(3)]
        slabs.append(rest[0] + pltpu.roll(rest[1], hl, 1))
        tails[p] = rest[2]
        if p == 1:
            slabs.append(tails[0] + pltpu.roll(tails[1], hl, 1))
        if p == 2:
            slabs.append(tails[2])
        for at, value in enumerate(slabs):
            value = value.reshape(units, SUB, LANE)
            q["wf"][at * units : (at + 1) * units] = value
            q["wb"][at * units : (at + 1) * units] = value.astype(BF16)
        used = len(slabs) * units
        total = q["wf"].shape[0]
        if total > used:
            q["wf"][used:] = jnp.zeros_like(q["wf"][used:])
            q["wb"][used:] = jnp.zeros_like(q["wb"][used:])
        half = total // 2
        q["half"], q["per"] = half, half // npl
        q["chunk"] = q["r3"].shape[1]
        q["pair"] = remote(
            q["wb"].at[pl.ds((1 - core) * half, half)], q["r1"],
            q["s"].at[0, 0], q["q"].at[0, 0], pair)
        q["pair"].start()

    def over_plane(p):
        q = parts[p]
        half = q["half"]
        q["pair"].wait()
        first = q["wf"][pl.ds(core * half, half)] + q["r1"][...].astype(F32)
        q["a1"][...] = first.reshape(q["a1"].shape)
        q["b1"][...] = first.reshape(q["a1"].shape).astype(BF16)
        q["plane"] = []
        for d in range(1, npl):
            index, where = plane_peer(d)
            copy = remote(q["b1"].at[index], q["r2"].at[d - 1],
                          q["s"].at[1, d - 1], q["q"].at[1, d - 1], where)
            copy.start()
            q["plane"].append(copy)

    def over_z(p):
        q = parts[p]
        per, chunk = q["per"], q["chunk"]
        for copy in q["plane"]:
            copy.wait()
        second = q["a1"][plane]
        for d in range(npl - 1):
            second = second + q["r2"][d].astype(F32)
        q["a2"][0:per] = second
        q["b2"][0:per] = second.astype(BF16)
        if nz * chunk > per:
            q["a2"][per:] = jnp.zeros_like(q["a2"][per:])
            q["b2"][per:] = jnp.zeros_like(q["b2"][per:])
        q["z"] = []
        for d in range(1, nz):
            index, where = z_peer(d)
            copy = remote(q["b2"].at[pl.ds(index * chunk, chunk)], q["r3"].at[d - 1],
                          q["s"].at[2, d - 1], q["q"].at[2, d - 1], where)
            copy.start()
            q["z"].append(copy)

    def z_return(p):
        q = parts[p]
        chunk = q["chunk"]
        for copy in q["z"]:
            copy.wait()
        mine = pl.ds(z * chunk, chunk)
        third = q["a2"][mine]
        for d in range(nz - 1):
            third = third + q["r3"][d].astype(F32)
        here = q["ag"].at[core, plane, mine]
        q["ag"][core, plane, mine] = (third * scale).astype(BF16)
        q["sent"] = []
        for d in range(1, nz):
            copy = remote(here, here, q["s"].at[3, d - 1], q["q"].at[3, d - 1], z_peer(d)[1])
            copy.start()
            q["sent"].append(copy)

    def plane_return(p):
        q = parts[p]
        chunk, per = q["chunk"], q["per"]
        for d in range(1, nz):
            source = lax.rem(z + nz - d, nz)
            there = q["ag"].at[core, plane, pl.ds(source * chunk, chunk)]
            remote(there, there, q["s"].at[3, d - 1], q["q"].at[3, d - 1], pair).wait_recv()
        here = q["ag"].at[core, plane, pl.ds(0, per)]
        for d in range(1, npl):
            copy = remote(here, here, q["s"].at[4, d - 1], q["q"].at[4, d - 1], plane_peer(d)[1])
            copy.start()
            q["sent"].append(copy)
        copy = remote(here, here, q["s"].at[5, 0], q["q"].at[5, 0], pair)
        copy.start()
        q["sent"].append(copy)

    def core_return(p):
        q = parts[p]
        for d in range(1, npl):
            source = lax.rem(plane + npl - d, npl)
            there = q["ag"].at[core, source, pl.ds(0, q["per"])]
            remote(there, there, q["s"].at[4, d - 1], q["q"].at[4, d - 1], pair).wait_recv()
            copy = remote(there, there, q["s"].at[5, d], q["q"].at[5, d], pair)
            copy.start()
            q["sent"].append(copy)

    def hand_out(p):
        q = parts[p]
        half, per = q["half"], q["per"]
        for d in range(npl):
            source = lax.rem(plane + npl - d, npl)
            there = q["ag"].at[1 - core, source, pl.ds(0, per)]
            remote(there, there, q["s"].at[5, d], q["q"].at[5, d], pair).wait_recv()

        def slab(at):
            found = []
            for t in range(at * units, (at + 1) * units):
                found.append(q["ag"][t // half, t % half // per, t % per])
            return jnp.concatenate(found, axis=0).astype(F32)

        for r in range(3):
            wgrad[r, p, :, 0:LANE] = slab(r)
        rest = slab(3)
        wgrad[0, p, :, LANE:ch] = rest[:, 0:hl]
        wgrad[1, p, :, LANE:ch] = pltpu.roll(rest, hl, 1)[:, 0:hl]
        if p == 1:
            rest = slab(4)
            wgrad[2, 0, :, LANE:ch] = rest[:, 0:hl]
            wgrad[2, 1, :, LANE:ch] = pltpu.roll(rest, hl, 1)[:, 0:hl]
        if p == 2:
            wgrad[2, 2, :, LANE:ch] = slab(4)[:, 0:hl]
        for r in range(3):
            for c in range(3):
                ready = c if r < 2 else max(c, 1)
                if ready == p:
                    store(wgrad.at[r, c], wgrad_hbm.at[r, c])

    nt = ((1,), (1,))
    add_up(0)
    add_up(1)
    over_plane(0)
    add_up(2)
    over_plane(1)
    pass_corners(1)
    over_plane(2)
    spread(1, wide_g, grad.astype(F32), (2, 1, 0))
    back = mm(wide_g[cols : cols + cells, :], k_bwd[1], nt)
    over_z(0)
    finish_halo(1)
    spread_halo(1, wide_g, (2, 1, 0))
    over_z(1)
    back = back + mm(wide_g[0:cells, :], k_bwd[2], nt)
    z_return(0)
    over_z(2)
    z_return(1)
    inner = mm(wide_g[2 * cols : cols + cells, :], k_bwd[0], nt)
    edge = mm(wide_g[cols + cells : 2 * cols + cells, :], k_north[...], nt)
    back = back + jnp.concatenate([inner, edge], axis=0)
    sgrad[...] = jnp.where(keep > 0, back, 0.0).astype(BF16).reshape(sgrad.shape)
    store(sgrad, sgrad_hbm)
    plane_return(0)
    z_return(2)
    plane_return(1)
    plane_return(2)
    core_return(0)
    core_return(1)
    hand_out(0)
    core_return(2)
    hand_out(1)
    hand_out(2)

    finish_sends(0)
    finish_sends(1)
    for q in parts:
        for copy in q["sent"]:
            copy.wait_send()
    for copy in stores:
        copy.wait()


def write_body(out, sgrad, wgrad, out_hbm, sgrad_hbm, wgrad_hbm, sems):
    copies = []
    for src, dst in ((out, out_hbm), (sgrad, sgrad_hbm)):
        step = src.shape[1] // 4
        for k in range(4):
            piece = (0, pl.ds(k * step, step))
            copies.append((src.at[piece], dst.at[piece]))
    for r in range(3):
        for c in range(3):
            copies.append((wgrad.at[r, c], wgrad_hbm.at[r, c]))
    copies = [pltpu.make_async_copy(a, b, sems.at[i]) for i, (a, b) in enumerate(copies)]
    for copy in copies:
        copy.start()
    for copy in copies:
        copy.wait()


def body(states, cotangent, weights, land_mask, ocean_tiles):
    n_lon, n_lat, n_dp = (lax.axis_size(a) for a in ("lon", "lat", "dp"))
    batch, rows, cols, ch = states.shape
    assert batch == 1 and ch == 192 and n_lon % 2 == 0 and cols & (cols - 1) == 0
    cells = rows * cols
    count = batch * n_dp * rows * n_lat * cols * n_lon
    wide = 2 * LANE
    nz, npl = n_lon // 2, n_lat * n_dp
    groups = 2 * npl
    tile = (SUB, LANE)
    vmem = pltpu.VMEM
    dma = pltpu.SemaphoreType.DMA

    def part_scratch(slabs):
        total = -(-slabs * (ch // SUB) // groups) * groups
        half = total // 2
        per = half // npl
        chunk = -(-per // nz)
        most = max(npl, nz)
        return {
            "wf": vmem((total,) + tile, F32),
            "wb": vmem((total,) + tile, BF16),
            "r1": vmem((half,) + tile, BF16),
            "a1": vmem((npl, per) + tile, F32),
            "b1": vmem((npl, per) + tile, BF16),
            "r2": vmem((npl - 1, per) + tile, BF16),
            "a2": vmem((nz * chunk,) + tile, F32),
            "b2": vmem((nz * chunk,) + tile, BF16),
            "r3": vmem((nz - 1, chunk) + tile, BF16),
            "ag": vmem((2, npl, nz * chunk) + tile, BF16),
            "s": dma((6, most)),
            "q": dma((6, most)),
        }

    scratch = [
        vmem(states.shape, BF16),
        vmem(states.shape, BF16),
        vmem(weights.shape, F32),
        vmem(states.shape, BF16),
        vmem(states.shape, BF16),
        vmem(weights.shape, BF16),
        vmem(land_mask.shape, jnp.int32),
        dma((4,)),
        dma((11,)),
        vmem((2, cells, ch), BF16),
        vmem((2, 2 * rows, ch), BF16),
        vmem((2, 2 * rows, ch), BF16),
        vmem((2, 2, cols + 2 * rows, ch), BF16),
        vmem((cells + 2 * cols, 3 * wide), BF16),
        vmem((cells + 2 * cols, 3 * wide), BF16),
        vmem((cells + 2 * cols, 3 * wide), BF16),
        vmem((3, 3 * wide, ch), BF16),
        vmem((3, ch, 3 * wide), BF16),
        vmem((ch, 3 * wide), BF16),
        vmem((3, wide, cells + 2 * cols), BF16),
        [part_scratch(slabs) for slabs in (4, 5, 5)],
        dma((2, 6)), dma((2, 6)),
    ]
    in_hbm = pl.BlockSpec(memory_space=pltpu.HBM)
    geo = (n_lon, n_lat, n_dp, 1.0 / math.sqrt(count))
    results = pl.pallas_call(
        functools.partial(kernel_body, geo),
        out_shape=(
            jax.ShapeDtypeStruct(states.shape, BF16),
            jax.ShapeDtypeStruct(states.shape, BF16),
            jax.ShapeDtypeStruct(weights.shape, F32),
        ),
        in_specs=[in_hbm] * 4 + [pl.BlockSpec(memory_space=pltpu.SMEM)],
        out_specs=(in_hbm,) * 3,
        scratch_shapes=scratch,
        compiler_params=pltpu.CompilerParams(
            collective_id=0, has_side_effects=True, vmem_limit_bytes=60 * 2**20
        ),
        cost_estimate=pl.CostEstimate(
            flops=54 * cells * ch * ch, bytes_accessed=5_000_000, transcendentals=cells * ch
        ),
    )(states, cotangent, weights, land_mask, ocean_tiles)
    return pl.pallas_call(
        write_body,
        out_shape=tuple(jax.ShapeDtypeStruct(v.shape, v.dtype) for v in results),
        in_specs=[in_hbm] * 3,
        out_specs=(in_hbm,) * 3,
        scratch_shapes=[dma((17,))],
        compiler_params=pltpu.CompilerParams(vmem_limit_bytes=60 * 2**20),
    )(*results)


def solution(mesh):
    in_specs = (
        P("dp", "lat", "lon", None),
        P("dp", "lat", "lon", None),
        P(),
        P("lat", "lon"),
        P("lat", "lon", None),
    )
    out_specs = (P("dp", "lat", "lon", None), P("dp", "lat", "lon", None), P())
    return jax.shard_map(body, mesh=mesh, in_specs=in_specs, out_specs=out_specs, check_vma=False)
```

```python
import functools
import math

import jax
import jax.numpy as jnp
from jax import lax
from jax.experimental import pallas as pl
from jax.experimental.pallas import tpu as pltpu
from jax.sharding import PartitionSpec as P

TS = 16
LANE = 128
SUB = 16
MESH = pl.DeviceIdType.MESH
F32 = jnp.float32
BF16 = jnp.bfloat16
NORTH, SOUTH = 0, 1


def iota(shape, axis):
    return lax.broadcasted_iota(jnp.int32, shape, axis)


def mm(a, b, dims=((1,), (0,))):
    return lax.dot_general(a, b, (dims, ((), ())), preferred_element_type=F32)


def onehot(cond):
    return jnp.where(cond, 1.0, 0.0).astype(BF16)


def kernel_body(
    geo,
    states_hbm, cotangent_hbm, weights_hbm, land_hbm, tiles,
    out_hbm, sgrad_hbm, wgrad_hbm,
    out, sgrad, wgrad, states, cotangent, weights, land, in_sem, out_sem,
    own, colsend, colrecv, halo, wide_x, wide_g, lag_g, k_fwd, k_bwd, k_north,
    x_turned, parts, hs_send, hs_recv,
):
    n_lon, n_lat, n_dp, scale = geo
    _, rows, cols, ch = states.shape
    cells = rows * cols
    wide = 2 * LANE
    lon, lat, dp = lax.axis_index("lon"), lax.axis_index("lat"), lax.axis_index("dp")
    core, z = lax.rem(lon, 2), lon // 2
    nz, npl = n_lon // 2, n_lat * n_dp
    plane = lat * n_dp + dp
    left = {"lon": lax.rem(lon + n_lon - 1, n_lon)}
    right = {"lon": lax.rem(lon + 1, n_lon)}
    top = lat == n_lat - 1
    mirror = {"lon": n_lon - 1 - lon}
    upward = {
        "lon": jnp.where(top, n_lon - 1 - lon, lon),
        "lat": jnp.where(top, lat, lat + 1),
    }
    up_slot = jnp.where(top, NORTH, SOUTH)
    downward = {"lat": jnp.maximum(lat - 1, 0)}
    pair = {"lon": lon + 1 - 2 * core}

    def plane_peer(d):
        index = lax.rem(plane + d, npl)
        return index, {"lat": index // n_dp, "dp": lax.rem(index, n_dp)}

    def z_peer(d):
        index = lax.rem(z + d, nz)
        return index, {"lon": index * 2 + core}

    def remote(src, dst, send, recv, where):
        return pltpu.make_async_remote_copy(
            src_ref=src, dst_ref=dst, send_sem=send, recv_sem=recv,
            device_id=where, device_id_type=MESH,
        )

    fetch = []
    for i, (src, dst) in enumerate((
        (land_hbm, land), (states_hbm, states), (weights_hbm, weights),
        (cotangent_hbm, cotangent),
    )):
        copy = pltpu.make_async_copy(src, dst, in_sem.at[i])
        copy.start()
        fetch.append(copy)
    stores = []

    def store(src, dst):
        copy = pltpu.make_async_copy(src, dst, out_sem.at[len(stores)])
        copy.start()
        stores.append(copy)

    barrier = pltpu.get_barrier_semaphore()

    def greet(where):
        pl.semaphore_signal(barrier, inc=1, device_id=where, device_id_type=MESH)

    greet(left)
    greet(right)
    for d in range(1, npl):
        greet(plane_peer(d)[1])
    for d in range(1, nz):
        greet(z_peer(d)[1])

    @pl.when(top)
    def _():
        greet(mirror)

    tile_cols = cols // TS
    number = iota((rows, cols), 0) // TS * tile_cols + iota((rows, cols), 1) // TS
    hit = number == tiles[0, 0, 0]
    for slot in range(1, tiles.shape[2]):
        hit = hit | (number == tiles[0, 0, slot])
    fetch[0].wait()
    keep_plane = jnp.where(hit, land[...], 0).astype(F32).astype(BF16)
    cell = iota((cells, rows), 0) - cols * iota((cells, rows), 1)
    by_row = mm(onehot((cell >= 0) & (cell < cols)), keep_plane)
    pos = iota((cells, cols), 0) & (cols - 1)
    by_cell = jnp.where(pos == iota((cells, cols), 1), by_row, 0.0).astype(BF16)
    keep = mm(by_cell, jnp.ones((cols, ch), BF16))
    column = iota((cells, ch), 0) & (cols - 1)
    at_first, at_last = column == 0, column == cols - 1
    first_of = onehot(cell == 0)
    last_of = onehot(cell == cols - 1)
    pick = iota((2 * rows, cells), 1) - jnp.where(
        iota((2 * rows, cells), 0) < rows,
        cols * iota((2 * rows, cells), 0),
        cols * (iota((2 * rows, cells), 0) - rows) + cols - 1,
    )
    pick = onehot(pick == 0)

    fetch[1].wait()
    masked = jnp.where(keep > 0, states[...].reshape(cells, ch).astype(F32), 0.0)
    own[0] = masked.astype(BF16)
    colsend[0] = mm(pick, own[0]).astype(BF16)

    @pl.when(lat == 0)
    def _():
        for which in range(2):
            halo[which, SOUTH] = jnp.zeros_like(halo[which, SOUTH])

    pl.semaphore_wait(barrier, 2 + (npl - 1) + (nz - 1) + jnp.where(top, 1, 0))

    def first_copies(w):
        send, recv = hs_send.at[w], hs_recv.at[w]
        to_left = remote(
            colsend.at[w, pl.ds(0, rows)], colrecv.at[w, pl.ds(rows, rows)],
            send.at[0], recv.at[0], left)
        to_right = remote(
            colsend.at[w, pl.ds(rows, rows)], colrecv.at[w, pl.ds(0, rows)],
            send.at[1], recv.at[1], right)
        up = remote(
            own.at[w, pl.ds(cells - cols, cols)], halo.at[w, up_slot, pl.ds(0, cols)],
            send.at[2], recv.at[2 + up_slot], upward)
        down = remote(
            own.at[w, pl.ds(0, cols)], halo.at[w, NORTH, pl.ds(0, cols)],
            send.at[3], recv.at[2 + NORTH], downward)
        return to_left, to_right, up, down

    def corner_copies(w):
        send, recv = hs_send.at[w], hs_recv.at[w]
        up = remote(
            colrecv.at[w], halo.at[w, up_slot, pl.ds(cols, 2 * rows)],
            send.at[4], recv.at[4 + up_slot], upward)
        down = remote(
            colrecv.at[w], halo.at[w, NORTH, pl.ds(cols, 2 * rows)],
            send.at[5], recv.at[4 + NORTH], downward)
        return up, down

    def start_first(w):
        to_left, to_right, up, down = first_copies(w)
        to_left.start()
        to_right.start()
        up.start()

        @pl.when(lat > 0)
        def _():
            down.start()

    def pass_corners(w):
        to_left, to_right, _, _ = first_copies(w)
        to_left.wait_recv()
        to_right.wait_recv()
        up, down = corner_copies(w)
        up.start()

        @pl.when(lat > 0)
        def _():
            down.start()

    def finish_halo(w):
        send, recv = hs_send.at[w], hs_recv.at[w]

        def arrived(slot):
            remote(own.at[w, pl.ds(0, cols)], halo.at[w, slot, pl.ds(0, cols)],
                   send.at[3], recv.at[2 + slot], downward).wait_recv()
            remote(colrecv.at[w], halo.at[w, slot, pl.ds(cols, 2 * rows)],
                   send.at[5], recv.at[4 + slot], downward).wait_recv()

        arrived(NORTH)

        @pl.when(lat > 0)
        def _():
            arrived(SOUTH)

    def finish_sends(w):
        to_left, to_right, up, down = first_copies(w)
        up2, down2 = corner_copies(w)
        for copy in (to_left, to_right, up, up2):
            copy.wait_send()

        @pl.when(lat > 0)
        def _():
            down.wait_send()
            down2.wait_send()

    def spread(w, ref, values, order):
        lane = [b * wide for b in order]
        body = pl.ds(0, cells)
        ref[body, lane[1] : lane[1] + ch] = own[w]
        low = mm(first_of, colrecv[w, :rows])
        ref[body, lane[0] : lane[0] + ch] = jnp.where(
            at_first, low, pltpu.roll(values, 1, 0)
        ).astype(BF16)
        high = mm(last_of, colrecv[w, rows:])
        ref[body, lane[2] : lane[2] + ch] = jnp.where(
            at_last, high, pltpu.roll(values, cells - 1, 0)
        ).astype(BF16)

    def spread_halo(w, ref, order):
        shape = (3 * cols, cols + 2 * rows)
        p, s = iota(shape, 0), iota(shape, 1)
        block = jnp.where(p >= cols, 1, 0) + jnp.where(p >= 2 * cols, 1, 0)
        east = p - cols * block + block - 1
        flip = jnp.where(top, 1, 0)
        for slot, at in ((NORTH, cells), (SOUTH, cells + cols)):
            if slot == NORTH:
                e = east + flip * (cols - 1 - 2 * east)
                edge = flip * (rows - 1)
            else:
                e, edge = east, rows - 1
            source = jnp.where(
                e < 0, cols + edge, jnp.where(e >= cols, cols + rows + edge, e))
            got = mm(onehot(s == source), halo[w, slot]).astype(BF16)
            for b in range(3):
                ref[at : at + cols, order[b] * wide : order[b] * wide + ch] = got[
                    b * cols : (b + 1) * cols
                ]

    start_first(0)
    fetch[2].wait()
    k_north[...] = jnp.zeros_like(k_north)
    for c in range(3):
        gap = pl.ds(c * wide + LANE, LANE)
        for ref in (wide_x, wide_g, lag_g):
            ref[:, gap] = jnp.zeros((ref.shape[0], LANE), BF16)
    for r, lo, hi in (
        (0, cells - cols, cells + cols), (1, cells, cells + 2 * cols),
        (2, 0, cols), (2, cells + cols, cells + 2 * cols),
    ):
        lag_g[lo:hi, r * wide : (r + 1) * wide] = jnp.zeros((hi - lo, wide), BF16)
    for r in range(3):
        k_bwd[r] = jnp.zeros_like(k_bwd[r])
        k_fwd[r] = jnp.zeros_like(k_fwd[r])
    for r in range(3):
        for c in range(3):
            k_fwd[r, c * wide : c * wide + ch, :] = weights[r, c]
            k_bwd[r, :, c * wide : c * wide + ch] = weights[r, c]

    @pl.when(top)
    def _():
        for c in range(3):
            k_north[:, c * wide : c * wide + ch] = weights[2, 2 - c]

    @pl.when(jnp.logical_not(top))
    def _():
        for c in range(3):
            k_north[:, c * wide : c * wide + ch] = weights[0, c]

    pass_corners(0)
    spread(0, wide_x, masked, (0, 1, 2))
    fetch[3].wait()

    def activate(lo, hi, pre):
        here = keep[lo:hi]
        sig = 1.0 / (1.0 + jnp.exp(-pre))
        first, last = lo // cols, hi // cols
        shape = (1, last - first, cols, ch)
        out[:, first:last] = (here * pre * sig).astype(BF16).reshape(shape)
        slope = sig * (1.0 + pre * (1.0 - sig))
        upstream = cotangent[:, first:last].reshape(hi - lo, ch).astype(F32)
        grad = (here * upstream * slope).astype(BF16)
        own[1, lo:hi] = grad
        lag_g[lo:hi, wide : wide + ch] = grad
        for r, step in ((0, -cols), (2, cols)):
            a, b = lo + step, hi + step
            if a < 0:
                lag_g[cells + cols : cells + 2 * cols, 0:ch] = grad[:cols]
                grad_in, a = grad[cols:], 0
            elif b > cells:
                lag_g[cells : cells + cols, 2 * wide : 2 * wide + ch] = grad[hi - lo - cols :]
                grad_in, b = grad[: hi - lo - cols], cells
            else:
                grad_in = grad
            if b > a:
                lag_g[a:b, r * wide : r * wide + ch] = grad_in

    for c in range(3):
        x_turned[c, :, 0:cells] = wide_x[0:cells, c * wide : (c + 1) * wide].T
    pre = mm(wide_x[0:cells, :], k_fwd[1])
    low = mm(wide_x[0 : cells - cols, :], k_fwd[0])
    high = mm(wide_x[cols:cells, :], k_fwd[2])
    mid = slice(cols, cells - cols)
    activate(cols, cells - cols, pre[mid] + low[: cells - 2 * cols] + high[cols:])
    finish_halo(0)
    spread_halo(0, wide_x, (0, 1, 2))
    for c in range(3):
        x_turned[c, :, cells:] = wide_x[cells:, c * wide : (c + 1) * wide].T
    low_edge = mm(wide_x[cells + cols :, :], k_fwd[0])
    high_edge = mm(wide_x[cells : cells + cols, :], k_fwd[2])
    activate(0, cols, pre[:cols] + high[:cols] + low_edge)
    activate(cells - cols, cells, pre[cells - cols :] + low[cells - 2 * cols :] + high_edge)
    colsend[1] = mm(pick, own[1]).astype(BF16)
    start_first(1)
    store(out, out_hbm)

    units = ch // SUB
    hl = LANE // 2
    tails = {}

    def add_up(p):
        q = parts[p]
        full = mm(x_turned[p], lag_g[...])
        band = full[:ch]
        slabs = [band[:, r * wide : r * wide + LANE] for r in range(3)]
        rest = [band[:, r * wide + LANE : (r + 1) * wide] for r in range(3)]
        slabs.append(rest[0] + pltpu.roll(rest[1], hl, 1))
        tails[p] = rest[2]
        if p == 1:
            slabs.append(tails[0] + pltpu.roll(tails[1], hl, 1))
        if p == 2:
            slabs.append(tails[2])
        for at, value in enumerate(slabs):
            value = value.reshape(units, SUB, LANE)
            q["wf"][at * units : (at + 1) * units] = value
            q["wb"][at * units : (at + 1) * units] = value.astype(BF16)
        used = len(slabs) * units
        total = q["wf"].shape[0]
        if total > used:
            q["wf"][used:] = jnp.zeros_like(q["wf"][used:])
            q["wb"][used:] = jnp.zeros_like(q["wb"][used:])
        half = total // 2
        q["half"], q["per"] = half, half // npl
        q["chunk"] = q["r3"].shape[1]
        q["pair"] = remote(
            q["wb"].at[pl.ds((1 - core) * half, half)], q["r1"],
            q["s"].at[0, 0], q["q"].at[0, 0], pair)
        q["pair"].start()

    def over_plane(p):
        q = parts[p]
        half = q["half"]
        q["pair"].wait()
        first = q["wf"][pl.ds(core * half, half)] + q["r1"][...].astype(F32)
        q["a1"][...] = first.reshape(q["a1"].shape)
        q["b1"][...] = first.reshape(q["a1"].shape).astype(BF16)
        q["plane"] = []
        for d in range(1, npl):
            index, where = plane_peer(d)
            copy = remote(q["b1"].at[index], q["r2"].at[d - 1],
                          q["s"].at[1, d - 1], q["q"].at[1, d - 1], where)
            copy.start()
            q["plane"].append(copy)

    def over_z(p):
        q = parts[p]
        per, chunk = q["per"], q["chunk"]
        for copy in q["plane"]:
            copy.wait()
        second = q["a1"][plane]
        for d in range(npl - 1):
            second = second + q["r2"][d].astype(F32)
        q["a2"][0:per] = second
        q["b2"][0:per] = second.astype(BF16)
        if nz * chunk > per:
            q["a2"][per:] = jnp.zeros_like(q["a2"][per:])
            q["b2"][per:] = jnp.zeros_like(q["b2"][per:])
        q["z"] = []
        for d in range(1, nz):
            index, where = z_peer(d)
            copy = remote(q["b2"].at[pl.ds(index * chunk, chunk)], q["r3"].at[d - 1],
                          q["s"].at[2, d - 1], q["q"].at[2, d - 1], where)
            copy.start()
            q["z"].append(copy)

    def z_return(p):
        q = parts[p]
        chunk = q["chunk"]
        for copy in q["z"]:
            copy.wait()
        mine = pl.ds(z * chunk, chunk)
        third = q["a2"][mine]
        for d in range(nz - 1):
            third = third + q["r3"][d].astype(F32)
        here = q["ag"].at[core, plane, mine]
        q["ag"][core, plane, mine] = (third * scale).astype(BF16)
        q["sent"] = []
        for d in range(1, nz):
            copy = remote(here, here, q["s"].at[3, d - 1], q["q"].at[3, d - 1], z_peer(d)[1])
            copy.start()
            q["sent"].append(copy)

    def plane_return(p):
        q = parts[p]
        chunk, per = q["chunk"], q["per"]
        for d in range(1, nz):
            source = lax.rem(z + nz - d, nz)
            there = q["ag"].at[core, plane, pl.ds(source * chunk, chunk)]
            remote(there, there, q["s"].at[3, d - 1], q["q"].at[3, d - 1], pair).wait_recv()
        here = q["ag"].at[core, plane, pl.ds(0, per)]
        for d in range(1, npl):
            copy = remote(here, here, q["s"].at[4, d - 1], q["q"].at[4, d - 1], plane_peer(d)[1])
            copy.start()
            q["sent"].append(copy)
        copy = remote(here, here, q["s"].at[5, 0], q["q"].at[5, 0], pair)
        copy.start()
        q["sent"].append(copy)

    def core_return(p):
        q = parts[p]
        for d in range(1, npl):
            source = lax.rem(plane + npl - d, npl)
            there = q["ag"].at[core, source, pl.ds(0, q["per"])]
            remote(there, there, q["s"].at[4, d - 1], q["q"].at[4, d - 1], pair).wait_recv()
            copy = remote(there, there, q["s"].at[5, d], q["q"].at[5, d], pair)
            copy.start()
            q["sent"].append(copy)

    def hand_out(p):
        q = parts[p]
        half, per = q["half"], q["per"]
        for d in range(npl):
            source = lax.rem(plane + npl - d, npl)
            there = q["ag"].at[1 - core, source, pl.ds(0, per)]
            remote(there, there, q["s"].at[5, d], q["q"].at[5, d], pair).wait_recv()

        def slab(at):
            found = []
            for t in range(at * units, (at + 1) * units):
                found.append(q["ag"][t // half, t % half // per, t % per])
            return jnp.concatenate(found, axis=0).astype(F32)

        for r in range(3):
            wgrad[r, p, :, 0:LANE] = slab(r)
        rest = slab(3)
        wgrad[0, p, :, LANE:ch] = rest[:, 0:hl]
        wgrad[1, p, :, LANE:ch] = pltpu.roll(rest, hl, 1)[:, 0:hl]
        if p == 1:
            rest = slab(4)
            wgrad[2, 0, :, LANE:ch] = rest[:, 0:hl]
            wgrad[2, 1, :, LANE:ch] = pltpu.roll(rest, hl, 1)[:, 0:hl]
        if p == 2:
            wgrad[2, 2, :, LANE:ch] = slab(4)[:, 0:hl]
        for r in range(3):
            for c in range(3):
                ready = c if r < 2 else max(c, 1)
                if ready == p:
                    store(wgrad.at[r, c], wgrad_hbm.at[r, c])

    nt = ((1,), (1,))
    add_up(0)
    add_up(1)
    over_plane(0)
    add_up(2)
    over_plane(1)
    pass_corners(1)
    over_plane(2)
    spread(1, wide_g, own[1].astype(F32), (2, 1, 0))
    back = mm(wide_g[0:cells, :], k_bwd[1], nt)
    over_z(0)
    finish_halo(1)
    spread_halo(1, wide_g, (2, 1, 0))
    over_z(1)
    below = mm(wide_g[0 : cells - cols, :], k_bwd[2], nt)
    below_edge = mm(wide_g[cells + cols :, :], k_bwd[2], nt)
    back = back + jnp.concatenate([below_edge, below], axis=0)
    z_return(0)
    over_z(2)
    z_return(1)
    inner = mm(wide_g[cols:cells, :], k_bwd[0], nt)
    edge = mm(wide_g[cells : cells + cols, :], k_north[...], nt)
    back = back + jnp.concatenate([inner, edge], axis=0)
    sgrad[...] = jnp.where(keep > 0, back, 0.0).astype(BF16).reshape(sgrad.shape)
    store(sgrad, sgrad_hbm)
    plane_return(0)
    z_return(2)
    plane_return(1)
    plane_return(2)
    core_return(0)
    core_return(1)
    hand_out(0)
    core_return(2)
    hand_out(1)
    hand_out(2)

    finish_sends(0)
    finish_sends(1)
    for q in parts:
        for copy in q["sent"]:
            copy.wait_send()
    for copy in stores:
        copy.wait()


def write_body(out, sgrad, wgrad, out_hbm, sgrad_hbm, wgrad_hbm, a, b, c, load, save):
    steps = []
    for src, mid, dst in ((out, a, out_hbm), (sgrad, b, sgrad_hbm)):
        step = src.shape[1] // 4
        for k in range(4):
            piece = (0, pl.ds(k * step, step))
            steps.append((src.at[piece], mid.at[piece], dst.at[piece]))
    for r in range(3):
        for k in range(3):
            steps.append((wgrad.at[r, k], c.at[r, k], wgrad_hbm.at[r, k]))
    loads = [pltpu.make_async_copy(x, y, load.at[i]) for i, (x, y, _) in enumerate(steps)]
    saves = [pltpu.make_async_copy(y, w, save.at[i]) for i, (_, y, w) in enumerate(steps)]
    for copy in loads:
        copy.start()
    for arrive, leave in zip(loads, saves):
        arrive.wait()
        leave.start()
    for copy in saves:
        copy.wait()


def body(states, cotangent, weights, land_mask, ocean_tiles):
    n_lon, n_lat, n_dp = (lax.axis_size(a) for a in ("lon", "lat", "dp"))
    batch, rows, cols, ch = states.shape
    assert batch == 1 and ch == 192 and n_lon % 2 == 0 and cols & (cols - 1) == 0
    cells = rows * cols
    count = batch * n_dp * rows * n_lat * cols * n_lon
    wide = 2 * LANE
    nz, npl = n_lon // 2, n_lat * n_dp
    groups = 2 * npl
    tile = (SUB, LANE)
    vmem = pltpu.VMEM
    dma = pltpu.SemaphoreType.DMA

    def part_scratch(slabs):
        total = -(-slabs * (ch // SUB) // groups) * groups
        half = total // 2
        per = half // npl
        chunk = -(-per // nz)
        most = max(npl, nz)
        return {
            "wf": vmem((total,) + tile, F32),
            "wb": vmem((total,) + tile, BF16),
            "r1": vmem((half,) + tile, BF16),
            "a1": vmem((npl, per) + tile, F32),
            "b1": vmem((npl, per) + tile, BF16),
            "r2": vmem((npl - 1, per) + tile, BF16),
            "a2": vmem((nz * chunk,) + tile, F32),
            "b2": vmem((nz * chunk,) + tile, BF16),
            "r3": vmem((nz - 1, chunk) + tile, BF16),
            "ag": vmem((2, npl, nz * chunk) + tile, BF16),
            "s": dma((6, most)),
            "q": dma((6, most)),
        }

    scratch = [
        vmem(states.shape, BF16),
        vmem(states.shape, BF16),
        vmem(weights.shape, F32),
        vmem(states.shape, BF16),
        vmem(states.shape, BF16),
        vmem(weights.shape, BF16),
        vmem(land_mask.shape, jnp.int32),
        dma((4,)),
        dma((11,)),
        vmem((2, cells, ch), BF16),
        vmem((2, 2 * rows, ch), BF16),
        vmem((2, 2 * rows, ch), BF16),
        vmem((2, 2, cols + 2 * rows, ch), BF16),
        vmem((cells + 2 * cols, 3 * wide), BF16),
        vmem((cells + 2 * cols, 3 * wide), BF16),
        vmem((cells + 2 * cols, 3 * wide), BF16),
        vmem((3, 3 * wide, ch), BF16),
        vmem((3, ch, 3 * wide), BF16),
        vmem((ch, 3 * wide), BF16),
        vmem((3, wide, cells + 2 * cols), BF16),
        [part_scratch(slabs) for slabs in (4, 5, 5)],
        dma((2, 6)), dma((2, 6)),
    ]
    in_hbm = pl.BlockSpec(memory_space=pltpu.HBM)
    geo = (n_lon, n_lat, n_dp, 1.0 / math.sqrt(count))
    results = pl.pallas_call(
        functools.partial(kernel_body, geo),
        out_shape=(
            jax.ShapeDtypeStruct(states.shape, BF16),
            jax.ShapeDtypeStruct(states.shape, BF16),
            jax.ShapeDtypeStruct(weights.shape, F32),
        ),
        in_specs=[in_hbm] * 4 + [pl.BlockSpec(memory_space=pltpu.SMEM)],
        out_specs=(in_hbm,) * 3,
        scratch_shapes=scratch,
        compiler_params=pltpu.CompilerParams(
            collective_id=0, has_side_effects=True, vmem_limit_bytes=60 * 2**20
        ),
        cost_estimate=pl.CostEstimate(
            flops=54 * cells * ch * ch, bytes_accessed=5_000_000, transcendentals=cells * ch
        ),
    )(states, cotangent, weights, land_mask, ocean_tiles)
    return pl.pallas_call(
        write_body,
        out_shape=tuple(jax.ShapeDtypeStruct(v.shape, v.dtype) for v in results),
        in_specs=[in_hbm] * 3,
        out_specs=(in_hbm,) * 3,
        scratch_shapes=[vmem(v.shape, v.dtype) for v in results] + [dma((17,)), dma((17,))],
        compiler_params=pltpu.CompilerParams(vmem_limit_bytes=60 * 2**20),
    )(*results)


def solution(mesh):
    in_specs = (
        P("dp", "lat", "lon", None),
        P("dp", "lat", "lon", None),
        P(),
        P("lat", "lon"),
        P("lat", "lon", None),
    )
    out_specs = (P("dp", "lat", "lon", None), P("dp", "lat", "lon", None), P())
    return jax.shard_map(body, mesh=mesh, in_specs=in_specs, out_specs=out_specs, check_vma=False)
```

```python
import functools
import math

import jax
import jax.numpy as jnp
from jax import lax
from jax.experimental import pallas as pl
from jax.experimental.pallas import tpu as pltpu
from jax.sharding import PartitionSpec as P

TS = 16
LANE = 128
SUB = 16
MESH = pl.DeviceIdType.MESH
F32 = jnp.float32
BF16 = jnp.bfloat16
NORTH, SOUTH = 0, 1


def iota(shape, axis):
    return lax.broadcasted_iota(jnp.int32, shape, axis)


def mm(a, b, dims=((1,), (0,))):
    return lax.dot_general(a, b, (dims, ((), ())), preferred_element_type=F32)


def onehot(cond):
    return jnp.where(cond, 1.0, 0.0).astype(BF16)


def kernel_body(
    geo,
    states_hbm, cotangent_hbm, weights_hbm, land_hbm, tiles_hbm,
    out, sgrad, wgrad,
    states, cotangent, weights, land, tiles, in_sem,
    own, colsend, colrecv, halo, wide_x, wide_g, lag_g, k_fwd, k_bwd, k_north,
    x_turned, parts, hs_send, hs_recv,
):
    n_lon, n_lat, n_dp, scale = geo
    _, rows, cols, ch = states.shape
    cells = rows * cols
    wide = 2 * LANE
    lon, lat, dp = lax.axis_index("lon"), lax.axis_index("lat"), lax.axis_index("dp")
    core, z = lax.rem(lon, 2), lon // 2
    nz, npl = n_lon // 2, n_lat * n_dp
    plane = lat * n_dp + dp
    left = {"lon": lax.rem(lon + n_lon - 1, n_lon)}
    right = {"lon": lax.rem(lon + 1, n_lon)}
    top = lat == n_lat - 1
    mirror = {"lon": n_lon - 1 - lon}
    upward = {
        "lon": jnp.where(top, n_lon - 1 - lon, lon),
        "lat": jnp.where(top, lat, lat + 1),
    }
    up_slot = jnp.where(top, NORTH, SOUTH)
    downward = {"lat": jnp.maximum(lat - 1, 0)}
    pair = {"lon": lon + 1 - 2 * core}

    def plane_peer(d):
        index = lax.rem(plane + d, npl)
        return index, {"lat": index // n_dp, "dp": lax.rem(index, n_dp)}

    def z_peer(d):
        index = lax.rem(z + d, nz)
        return index, {"lon": index * 2 + core}

    def remote(src, dst, send, recv, where):
        return pltpu.make_async_remote_copy(
            src_ref=src, dst_ref=dst, send_sem=send, recv_sem=recv,
            device_id=where, device_id_type=MESH,
        )

    fetch = []
    for i, (src, dst) in enumerate((
        (land_hbm, land), (states_hbm, states), (weights_hbm, weights),
        (cotangent_hbm, cotangent), (tiles_hbm, tiles),
    )):
        copy = pltpu.make_async_copy(src, dst, in_sem.at[i])
        copy.start()
        fetch.append(copy)
    barrier = pltpu.get_barrier_semaphore()

    def greet(where):
        pl.semaphore_signal(barrier, inc=1, device_id=where, device_id_type=MESH)

    greet(left)
    greet(right)
    for d in range(1, npl):
        greet(plane_peer(d)[1])
    for d in range(1, nz):
        greet(z_peer(d)[1])

    @pl.when(top)
    def _():
        greet(mirror)

    tile_cols = cols // TS
    number = iota((rows, cols), 0) // TS * tile_cols + iota((rows, cols), 1) // TS
    fetch[0].wait()
    fetch[4].wait()
    hit = number == tiles[0, :, 0:1]
    for slot in range(1, tiles.shape[2]):
        hit = hit | (number == tiles[0, :, slot : slot + 1])
    keep_plane = jnp.where(hit, land[...], 0).astype(F32).astype(BF16)
    cell = iota((cells, rows), 0) - cols * iota((cells, rows), 1)
    by_row = mm(onehot((cell >= 0) & (cell < cols)), keep_plane)
    pos = iota((cells, cols), 0) & (cols - 1)
    by_cell = jnp.where(pos == iota((cells, cols), 1), by_row, 0.0).astype(BF16)
    keep = mm(by_cell, jnp.ones((cols, ch), BF16))
    pick = iota((2 * rows, cells), 1) - jnp.where(
        iota((2 * rows, cells), 0) < rows,
        cols * iota((2 * rows, cells), 0),
        cols * (iota((2 * rows, cells), 0) - rows) + cols - 1,
    )
    pick = onehot(pick == 0)

    fetch[1].wait()
    masked = jnp.where(keep > 0, states[...].reshape(cells, ch).astype(F32), 0.0)
    own[0] = masked.astype(BF16)
    colsend[0] = mm(pick, own[0]).astype(BF16)

    @pl.when(lat == 0)
    def _():
        for which in range(2):
            halo[which, SOUTH] = jnp.zeros_like(halo[which, SOUTH])

    pl.semaphore_wait(barrier, 2 + (npl - 1) + (nz - 1) + jnp.where(top, 1, 0))

    def first_copies(w):
        send, recv = hs_send.at[w], hs_recv.at[w]
        to_left = remote(
            colsend.at[w, pl.ds(0, rows)], colrecv.at[w, pl.ds(rows, rows)],
            send.at[0], recv.at[0], left)
        to_right = remote(
            colsend.at[w, pl.ds(rows, rows)], colrecv.at[w, pl.ds(0, rows)],
            send.at[1], recv.at[1], right)
        up = remote(
            own.at[w, pl.ds(cells - cols, cols)], halo.at[w, up_slot, pl.ds(0, cols)],
            send.at[2], recv.at[2 + up_slot], upward)
        down = remote(
            own.at[w, pl.ds(0, cols)], halo.at[w, NORTH, pl.ds(0, cols)],
            send.at[3], recv.at[2 + NORTH], downward)
        return to_left, to_right, up, down

    def corner_copies(w):
        send, recv = hs_send.at[w], hs_recv.at[w]
        up = remote(
            colrecv.at[w], halo.at[w, up_slot, pl.ds(cols, 2 * rows)],
            send.at[4], recv.at[4 + up_slot], upward)
        down = remote(
            colrecv.at[w], halo.at[w, NORTH, pl.ds(cols, 2 * rows)],
            send.at[5], recv.at[4 + NORTH], downward)
        return up, down

    def start_first(w):
        to_left, to_right, up, down = first_copies(w)
        to_left.start()
        to_right.start()
        up.start()

        @pl.when(lat > 0)
        def _():
            down.start()

    def pass_corners(w):
        to_left, to_right, _, _ = first_copies(w)
        to_left.wait_recv()
        to_right.wait_recv()
        up, down = corner_copies(w)
        up.start()

        @pl.when(lat > 0)
        def _():
            down.start()

    def finish_halo(w):
        send, recv = hs_send.at[w], hs_recv.at[w]

        def arrived(slot):
            remote(own.at[w, pl.ds(0, cols)], halo.at[w, slot, pl.ds(0, cols)],
                   send.at[3], recv.at[2 + slot], downward).wait_recv()
            remote(colrecv.at[w], halo.at[w, slot, pl.ds(cols, 2 * rows)],
                   send.at[5], recv.at[4 + slot], downward).wait_recv()

        arrived(NORTH)

        @pl.when(lat > 0)
        def _():
            arrived(SOUTH)

    def finish_sends(w):
        to_left, to_right, up, down = first_copies(w)
        up2, down2 = corner_copies(w)
        for copy in (to_left, to_right, up, up2):
            copy.wait_send()

        @pl.when(lat > 0)
        def _():
            down.wait_send()
            down2.wait_send()

    def spread(w, ref, values, order):
        lane = [b * wide for b in order]
        body = pl.ds(0, cells)
        ref[body, lane[1] : lane[1] + ch] = own[w]
        ref[body, lane[0] : lane[0] + ch] = pltpu.roll(values, 1, 0).astype(BF16)
        ref[body, lane[2] : lane[2] + ch] = pltpu.roll(values, cells - 1, 0).astype(BF16)

    def patch(w, ref, order):
        line = iota((SUB, ch), 0)
        margin = colrecv[w].astype(F32)
        for j in range(rows):
            for b, at, spot in ((0, j * cols, 0), (2, (j + 1) * cols - SUB, SUB - 1)):
                lane = order[b] * wide
                here = (slice(at, at + SUB), slice(lane, lane + ch))
                value = margin[j + (rows if b else 0)][None]
                ref[here] = jnp.where(
                    line == spot, value, ref[here].astype(F32)
                ).astype(BF16)

    def spread_halo(w, ref, order):
        shape = (3 * cols, cols + 2 * rows)
        p, s = iota(shape, 0), iota(shape, 1)
        block = jnp.where(p >= cols, 1, 0) + jnp.where(p >= 2 * cols, 1, 0)
        east = p - cols * block + block - 1
        flip = jnp.where(top, 1, 0)
        for slot, at in ((NORTH, cells), (SOUTH, cells + cols)):
            if slot == NORTH:
                e = east + flip * (cols - 1 - 2 * east)
                edge = flip * (rows - 1)
            else:
                e, edge = east, rows - 1
            source = jnp.where(
                e < 0, cols + edge, jnp.where(e >= cols, cols + rows + edge, e))
            got = mm(onehot(s == source), halo[w, slot]).astype(BF16)
            for b in range(3):
                ref[at : at + cols, order[b] * wide : order[b] * wide + ch] = got[
                    b * cols : (b + 1) * cols
                ]

    start_first(0)
    fetch[2].wait()
    k_north[...] = jnp.zeros_like(k_north)
    for c in range(3):
        gap = pl.ds(c * wide + LANE, LANE)
        for ref in (wide_x, wide_g, lag_g):
            ref[:, gap] = jnp.zeros((ref.shape[0], LANE), BF16)
    for r, lo, hi in (
        (0, cells - cols, cells + cols), (1, cells, cells + 2 * cols),
        (2, 0, cols), (2, cells + cols, cells + 2 * cols),
    ):
        lag_g[lo:hi, r * wide : (r + 1) * wide] = jnp.zeros((hi - lo, wide), BF16)
    for r in range(3):
        k_bwd[r] = jnp.zeros_like(k_bwd[r])
        for c in range(3):
            k_fwd[r, c * wide + ch : (c + 1) * wide, :] = jnp.zeros((wide - ch, ch), BF16)
    for r in range(3):
        for c in range(3):
            k_fwd[r, c * wide : c * wide + ch, :] = weights[r, c]
            k_bwd[r, :, c * wide : c * wide + ch] = weights[r, c]

    @pl.when(top)
    def _():
        for c in range(3):
            k_north[:, c * wide : c * wide + ch] = weights[2, 2 - c]

    @pl.when(jnp.logical_not(top))
    def _():
        for c in range(3):
            k_north[:, c * wide : c * wide + ch] = weights[0, c]

    spread(0, wide_x, masked, (0, 1, 2))
    pass_corners(0)
    patch(0, wide_x, (0, 1, 2))
    fetch[3].wait()

    def activate(lo, hi, pre):
        here = keep[lo:hi]
        sig = 0.5 * jnp.tanh(0.5 * pre) + 0.5
        first, last = lo // cols, hi // cols
        shape = (1, last - first, cols, ch)
        out[:, first:last] = (here * pre * sig).astype(BF16).reshape(shape)
        slope = sig * (1.0 + pre * (1.0 - sig))
        upstream = cotangent[:, first:last].reshape(hi - lo, ch).astype(F32)
        grad = (here * upstream * slope).astype(BF16)
        own[1, lo:hi] = grad
        lag_g[lo:hi, wide : wide + ch] = grad
        for r, step in ((0, -cols), (2, cols)):
            a, b = lo + step, hi + step
            if a < 0:
                lag_g[cells + cols : cells + 2 * cols, 0:ch] = grad[:cols]
                grad_in, a = grad[cols:], 0
            elif b > cells:
                lag_g[cells : cells + cols, 2 * wide : 2 * wide + ch] = grad[hi - lo - cols :]
                grad_in, b = grad[: hi - lo - cols], cells
            else:
                grad_in = grad
            if b > a:
                lag_g[a:b, r * wide : r * wide + ch] = grad_in

    for c in range(3):
        x_turned[c, :, 0:cells] = wide_x[0:cells, c * wide : (c + 1) * wide].T
    pre = mm(wide_x[0:cells, :], k_fwd[1])
    low = mm(wide_x[0 : cells - cols, :], k_fwd[0])
    high = mm(wide_x[cols:cells, :], k_fwd[2])
    mid = slice(cols, cells - cols)
    activate(cols, cells - cols, pre[mid] + low[: cells - 2 * cols] + high[cols:])
    finish_halo(0)
    spread_halo(0, wide_x, (0, 1, 2))
    for c in range(3):
        x_turned[c, :, cells:] = wide_x[cells:, c * wide : (c + 1) * wide].T
    low_edge = mm(wide_x[cells + cols :, :], k_fwd[0])
    high_edge = mm(wide_x[cells : cells + cols, :], k_fwd[2])
    activate(0, cols, pre[:cols] + high[:cols] + low_edge)
    activate(cells - cols, cells, pre[cells - cols :] + low[cells - 2 * cols :] + high_edge)
    colsend[1] = mm(pick, own[1]).astype(BF16)
    start_first(1)

    units = ch // SUB
    hl = LANE // 2
    tails = {}

    def add_up(p):
        q = parts[p]
        full = mm(x_turned[p], lag_g[...])
        band = full[:ch]
        slabs = [band[:, r * wide : r * wide + LANE] for r in range(3)]
        rest = [band[:, r * wide + LANE : (r + 1) * wide] for r in range(3)]
        slabs.append(rest[0] + pltpu.roll(rest[1], hl, 1))
        tails[p] = rest[2]
        if p == 1:
            slabs.append(tails[0] + pltpu.roll(tails[1], hl, 1))
        if p == 2:
            slabs.append(tails[2])
        for at, value in enumerate(slabs):
            value = value.reshape(units, SUB, LANE)
            q["wf"][at * units : (at + 1) * units] = value
            q["wb"][at * units : (at + 1) * units] = value.astype(BF16)
        used = len(slabs) * units
        total = q["wf"].shape[0]
        if total > used:
            q["wf"][used:] = jnp.zeros_like(q["wf"][used:])
            q["wb"][used:] = jnp.zeros_like(q["wb"][used:])
        half = total // 2
        q["half"], q["per"] = half, half // npl
        q["chunk"] = q["r3"].shape[1]
        q["pair"] = remote(
            q["wb"].at[pl.ds((1 - core) * half, half)], q["r1"],
            q["s"].at[0, 0], q["q"].at[0, 0], pair)
        q["pair"].start()

    def over_plane(p):
        q = parts[p]
        half = q["half"]
        q["pair"].wait()
        first = q["wf"][pl.ds(core * half, half)] + q["r1"][...].astype(F32)
        q["a1"][...] = first.reshape(q["a1"].shape)
        q["b1"][...] = first.reshape(q["a1"].shape).astype(BF16)
        q["plane"] = []
        for d in range(1, npl):
            index, where = plane_peer(d)
            copy = remote(q["b1"].at[index], q["r2"].at[d - 1],
                          q["s"].at[1, d - 1], q["q"].at[1, d - 1], where)
            copy.start()
            q["plane"].append(copy)

    def over_z(p):
        q = parts[p]
        per, chunk = q["per"], q["chunk"]
        for copy in q["plane"]:
            copy.wait()
        second = q["a1"][plane]
        for d in range(npl - 1):
            second = second + q["r2"][d].astype(F32)
        q["a2"][0:per] = second
        q["b2"][0:per] = second.astype(BF16)
        if nz * chunk > per:
            q["a2"][per:] = jnp.zeros_like(q["a2"][per:])
            q["b2"][per:] = jnp.zeros_like(q["b2"][per:])
        q["z"] = []
        for d in range(1, nz):
            index, where = z_peer(d)
            copy = remote(q["b2"].at[pl.ds(index * chunk, chunk)], q["r3"].at[d - 1],
                          q["s"].at[2, d - 1], q["q"].at[2, d - 1], where)
            copy.start()
            q["z"].append(copy)

    def z_return(p):
        q = parts[p]
        chunk = q["chunk"]
        for copy in q["z"]:
            copy.wait()
        mine = pl.ds(z * chunk, chunk)
        third = q["a2"][mine]
        for d in range(nz - 1):
            third = third + q["r3"][d].astype(F32)
        here = q["ag"].at[core, plane, mine]
        q["ag"][core, plane, mine] = (third * scale).astype(BF16)
        q["sent"] = []
        for d in range(1, nz):
            copy = remote(here, here, q["s"].at[3, d - 1], q["q"].at[3, d - 1], z_peer(d)[1])
            copy.start()
            q["sent"].append(copy)

    def plane_return(p):
        q = parts[p]
        chunk, per = q["chunk"], q["per"]
        for d in range(1, nz):
            source = lax.rem(z + nz - d, nz)
            there = q["ag"].at[core, plane, pl.ds(source * chunk, chunk)]
            remote(there, there, q["s"].at[3, d - 1], q["q"].at[3, d - 1], pair).wait_recv()
        here = q["ag"].at[core, plane, pl.ds(0, per)]
        for d in range(1, npl):
            copy = remote(here, here, q["s"].at[4, d - 1], q["q"].at[4, d - 1], plane_peer(d)[1])
            copy.start()
            q["sent"].append(copy)
        copy = remote(here, here, q["s"].at[5, 0], q["q"].at[5, 0], pair)
        copy.start()
        q["sent"].append(copy)

    def core_return(p):
        q = parts[p]
        for d in range(1, npl):
            source = lax.rem(plane + npl - d, npl)
            there = q["ag"].at[core, source, pl.ds(0, q["per"])]
            remote(there, there, q["s"].at[4, d - 1], q["q"].at[4, d - 1], pair).wait_recv()
            copy = remote(there, there, q["s"].at[5, d], q["q"].at[5, d], pair)
            copy.start()
            q["sent"].append(copy)

    def hand_out(p):
        q = parts[p]
        half, per = q["half"], q["per"]
        for d in range(npl):
            source = lax.rem(plane + npl - d, npl)
            there = q["ag"].at[1 - core, source, pl.ds(0, per)]
            remote(there, there, q["s"].at[5, d], q["q"].at[5, d], pair).wait_recv()

        def slab(at):
            found = []
            for t in range(at * units, (at + 1) * units):
                found.append(q["ag"][t // half, t % half // per, t % per])
            return jnp.concatenate(found, axis=0).astype(F32)

        for r in range(3):
            wgrad[r, p, :, 0:LANE] = slab(r)
        rest = slab(3)
        wgrad[0, p, :, LANE:ch] = rest[:, 0:hl]
        wgrad[1, p, :, LANE:ch] = pltpu.roll(rest, hl, 1)[:, 0:hl]
        if p == 1:
            rest = slab(4)
            wgrad[2, 0, :, LANE:ch] = rest[:, 0:hl]
            wgrad[2, 1, :, LANE:ch] = pltpu.roll(rest, hl, 1)[:, 0:hl]
        if p == 2:
            wgrad[2, 2, :, LANE:ch] = slab(4)[:, 0:hl]

    nt = ((1,), (1,))
    add_up(0)
    add_up(1)
    over_plane(0)
    add_up(2)
    over_plane(1)
    pass_corners(1)
    spread(1, wide_g, own[1].astype(F32), (2, 1, 0))
    over_plane(2)
    patch(1, wide_g, (2, 1, 0))
    back = mm(wide_g[0:cells, :], k_bwd[1], nt)
    over_z(0)
    finish_halo(1)
    spread_halo(1, wide_g, (2, 1, 0))
    over_z(1)
    below = mm(wide_g[0 : cells - cols, :], k_bwd[2], nt)
    below_edge = mm(wide_g[cells + cols :, :], k_bwd[2], nt)
    back = back + jnp.concatenate([below_edge, below], axis=0)
    z_return(0)
    over_z(2)
    z_return(1)
    inner = mm(wide_g[cols:cells, :], k_bwd[0], nt)
    edge = mm(wide_g[cells : cells + cols, :], k_north[...], nt)
    back = back + jnp.concatenate([inner, edge], axis=0)
    sgrad[...] = jnp.where(keep > 0, back, 0.0).astype(BF16).reshape(sgrad.shape)
    plane_return(0)
    z_return(2)
    plane_return(1)
    plane_return(2)
    core_return(0)
    core_return(1)
    hand_out(0)
    core_return(2)
    hand_out(1)
    hand_out(2)

    finish_sends(0)
    finish_sends(1)
    for q in parts:
        for copy in q["sent"]:
            copy.wait_send()


def write_body(out, sgrad, wgrad, out_hbm, sgrad_hbm, wgrad_hbm, save):
    steps = []
    for src, dst in ((out, out_hbm), (sgrad, sgrad_hbm)):
        step = src.shape[1] // 4
        for k in range(4):
            piece = (0, pl.ds(k * step, step))
            steps.append((src.at[piece], dst.at[piece]))
    for r in range(3):
        for k in range(3):
            steps.append((wgrad.at[r, k], wgrad_hbm.at[r, k]))
    saves = [pltpu.make_async_copy(y, w, save.at[i]) for i, (y, w) in enumerate(steps)]
    for copy in saves:
        copy.start()
    for copy in saves:
        copy.wait()


def body(states, cotangent, weights, land_mask, ocean_tiles):
    n_lon, n_lat, n_dp = (lax.axis_size(a) for a in ("lon", "lat", "dp"))
    batch, rows, cols, ch = states.shape
    assert batch == 1 and ch == 192 and n_lon % 2 == 0 and cols & (cols - 1) == 0
    cells = rows * cols
    count = batch * n_dp * rows * n_lat * cols * n_lon
    wide = 2 * LANE
    nz, npl = n_lon // 2, n_lat * n_dp
    groups = 2 * npl
    tile = (SUB, LANE)
    vmem = pltpu.VMEM
    dma = pltpu.SemaphoreType.DMA

    def part_scratch(slabs):
        total = -(-slabs * (ch // SUB) // groups) * groups
        half = total // 2
        per = half // npl
        chunk = -(-per // nz)
        most = max(npl, nz)
        return {
            "wf": vmem((total,) + tile, F32),
            "wb": vmem((total,) + tile, BF16),
            "r1": vmem((half,) + tile, BF16),
            "a1": vmem((npl, per) + tile, F32),
            "b1": vmem((npl, per) + tile, BF16),
            "r2": vmem((npl - 1, per) + tile, BF16),
            "a2": vmem((nz * chunk,) + tile, F32),
            "b2": vmem((nz * chunk,) + tile, BF16),
            "r3": vmem((nz - 1, chunk) + tile, BF16),
            "ag": vmem((2, npl, nz * chunk) + tile, BF16),
            "s": dma((6, most)),
            "q": dma((6, most)),
        }

    scratch = [
        vmem(states.shape, BF16),
        vmem(states.shape, BF16),
        vmem(weights.shape, BF16),
        vmem(land_mask.shape, jnp.int32),
        vmem(ocean_tiles.shape, jnp.int32),
        dma((5,)),
        vmem((2, cells, ch), BF16),
        vmem((2, 2 * rows, ch), BF16),
        vmem((2, 2 * rows, ch), BF16),
        vmem((2, 2, cols + 2 * rows, ch), BF16),
        vmem((cells + 2 * cols, 3 * wide), BF16),
        vmem((cells + 2 * cols, 3 * wide), BF16),
        vmem((cells + 2 * cols, 3 * wide), BF16),
        vmem((3, 3 * wide, ch), BF16),
        vmem((3, ch, 3 * wide), BF16),
        vmem((ch, 3 * wide), BF16),
        vmem((3, wide, cells + 2 * cols), BF16),
        [part_scratch(slabs) for slabs in (4, 5, 5)],
        dma((2, 6)), dma((2, 6)),
    ]
    in_vmem = pl.BlockSpec(memory_space=pltpu.VMEM)
    in_hbm = pl.BlockSpec(memory_space=pltpu.HBM)
    geo = (n_lon, n_lat, n_dp, 1.0 / math.sqrt(count))
    pinned = [
        pltpu.with_memory_space_constraint(v, pltpu.HBM)
        for v in (states, cotangent, weights, land_mask, ocean_tiles)
    ]
    results = pl.pallas_call(
        functools.partial(kernel_body, geo),
        out_shape=(
            vmem(states.shape, BF16),
            vmem(states.shape, BF16),
            vmem(weights.shape, F32),
        ),
        in_specs=[in_hbm] * 5,
        out_specs=(in_vmem,) * 3,
        scratch_shapes=scratch,
        compiler_params=pltpu.CompilerParams(
            collective_id=0, has_side_effects=True, vmem_limit_bytes=40 * 2**20
        ),
        cost_estimate=pl.CostEstimate(
            flops=54 * cells * ch * ch, bytes_accessed=5_000_000, transcendentals=cells * ch
        ),
    )(*pinned)
    return pl.pallas_call(
        write_body,
        out_shape=tuple(jax.ShapeDtypeStruct(v.shape, v.dtype) for v in results),
        in_specs=[in_vmem] * 3,
        out_specs=(in_hbm,) * 3,
        scratch_shapes=[dma((17,))],
        compiler_params=pltpu.CompilerParams(vmem_limit_bytes=2**20),
    )(*results)


def solution(mesh):
    in_specs = (
        P("dp", "lat", "lon", None),
        P("dp", "lat", "lon", None),
        P(),
        P("lat", "lon"),
        P("lat", "lon", None),
    )
    out_specs = (P("dp", "lat", "lon", None), P("dp", "lat", "lon", None), P())
    return jax.shard_map(body, mesh=mesh, in_specs=in_specs, out_specs=out_specs, check_vma=False)
```

```python
import functools
import math

import jax
import jax.numpy as jnp
from jax import lax
from jax.experimental import pallas as pl
from jax.experimental.pallas import tpu as pltpu
from jax.sharding import PartitionSpec as P

TS = 16
LANE = 128
SUB = 16
MESH = pl.DeviceIdType.MESH
F32 = jnp.float32
BF16 = jnp.bfloat16
NORTH, SOUTH = 0, 1


def iota(shape, axis):
    return lax.broadcasted_iota(jnp.int32, shape, axis)


def mm(a, b, dims=((1,), (0,))):
    return lax.dot_general(a, b, (dims, ((), ())), preferred_element_type=F32)


def onehot(cond):
    return jnp.where(cond, 1.0, 0.0).astype(BF16)


def kernel_body(
    geo,
    states_hbm, cotangent_hbm, weights_hbm, land_hbm, tiles_hbm,
    out, sgrad, wgrad,
    states, cotangent, weights, land, tiles, in_sem,
    own, colsend, colrecv, halo, wide_x, wide_g, lag_g, k_fwd, k_bwd, k_north,
    x_turned, parts, hs_send, hs_recv,
):
    n_lon, n_lat, n_dp, scale = geo
    _, rows, cols, ch = states.shape
    cells = rows * cols
    wide = 2 * LANE
    lon, lat, dp = lax.axis_index("lon"), lax.axis_index("lat"), lax.axis_index("dp")
    core, z = lax.rem(lon, 2), lon // 2
    nz, npl = n_lon // 2, n_lat * n_dp
    plane = lat * n_dp + dp
    left = {"lon": lax.rem(lon + n_lon - 1, n_lon)}
    right = {"lon": lax.rem(lon + 1, n_lon)}
    top = lat == n_lat - 1
    mirror = {"lon": n_lon - 1 - lon}
    upward = {
        "lon": jnp.where(top, n_lon - 1 - lon, lon),
        "lat": jnp.where(top, lat, lat + 1),
    }
    up_slot = jnp.where(top, NORTH, SOUTH)
    downward = {"lat": jnp.maximum(lat - 1, 0)}
    pair = {"lon": lon + 1 - 2 * core}

    def plane_peer(d):
        index = lax.rem(plane + d, npl)
        return index, {"lat": index // n_dp, "dp": lax.rem(index, n_dp)}

    def z_peer(d):
        index = lax.rem(z + d, nz)
        return index, {"lon": index * 2 + core}

    def remote(src, dst, send, recv, where):
        return pltpu.make_async_remote_copy(
            src_ref=src, dst_ref=dst, send_sem=send, recv_sem=recv,
            device_id=where, device_id_type=MESH,
        )

    fetch = []
    for i, (src, dst) in enumerate((
        (land_hbm, land), (tiles_hbm, tiles), (states_hbm, states),
        (weights_hbm, weights), (cotangent_hbm, cotangent),
    )):
        copy = pltpu.make_async_copy(src, dst, in_sem.at[i])
        copy.start()
        fetch.append(copy)
    barrier = pltpu.get_barrier_semaphore()

    def greet(where):
        pl.semaphore_signal(barrier, inc=1, device_id=where, device_id_type=MESH)

    greet(left)
    greet(right)
    for d in range(1, npl):
        greet(plane_peer(d)[1])
    for d in range(1, nz):
        greet(z_peer(d)[1])

    @pl.when(top)
    def _():
        greet(mirror)

    tile_cols = cols // TS
    number = iota((rows, cols), 0) // TS * tile_cols + iota((rows, cols), 1) // TS
    cell = iota((cells, rows), 0) - cols * iota((cells, rows), 1)
    in_row = onehot((cell >= 0) & (cell < cols))
    pick = iota((2 * rows, cells), 1) - jnp.where(
        iota((2 * rows, cells), 0) < rows,
        cols * iota((2 * rows, cells), 0),
        cols * (iota((2 * rows, cells), 0) - rows) + cols - 1,
    )
    pick = onehot(pick == 0)
    fetch[0].wait()
    fetch[1].wait()
    hit = number == tiles[0, :, 0:1]
    for slot in range(1, tiles.shape[2]):
        hit = hit | (number == tiles[0, :, slot : slot + 1])
    keep_plane = jnp.where(hit, land[...], 0).astype(F32).astype(BF16)
    by_row = mm(in_row, keep_plane)
    pos = iota((cells, cols), 0) & (cols - 1)
    by_cell = jnp.where(pos == iota((cells, cols), 1), by_row, 0.0).astype(BF16)
    keep = mm(by_cell, jnp.ones((cols, ch), BF16))
    fetch[2].wait()
    masked = jnp.where(keep > 0, states[...].reshape(cells, ch).astype(F32), 0.0)
    own[0] = masked.astype(BF16)
    colsend[0] = mm(pick, own[0]).astype(BF16)

    @pl.when(lat == 0)
    def _():
        for which in range(2):
            halo[which, SOUTH] = jnp.zeros_like(halo[which, SOUTH])

    pl.semaphore_wait(barrier, 2 + (npl - 1) + (nz - 1) + jnp.where(top, 1, 0))

    def first_copies(w):
        send, recv = hs_send.at[w], hs_recv.at[w]
        to_left = remote(
            colsend.at[w, pl.ds(0, rows)], colrecv.at[w, pl.ds(rows, rows)],
            send.at[0], recv.at[0], left)
        to_right = remote(
            colsend.at[w, pl.ds(rows, rows)], colrecv.at[w, pl.ds(0, rows)],
            send.at[1], recv.at[1], right)
        up = remote(
            own.at[w, pl.ds(cells - cols, cols)], halo.at[w, up_slot, pl.ds(0, cols)],
            send.at[2], recv.at[2 + up_slot], upward)
        down = remote(
            own.at[w, pl.ds(0, cols)], halo.at[w, NORTH, pl.ds(0, cols)],
            send.at[3], recv.at[2 + NORTH], downward)
        return to_left, to_right, up, down

    def corner_copies(w):
        send, recv = hs_send.at[w], hs_recv.at[w]
        up = remote(
            colrecv.at[w], halo.at[w, up_slot, pl.ds(cols, 2 * rows)],
            send.at[4], recv.at[4 + up_slot], upward)
        down = remote(
            colrecv.at[w], halo.at[w, NORTH, pl.ds(cols, 2 * rows)],
            send.at[5], recv.at[4 + NORTH], downward)
        return up, down

    def start_first(w):
        to_left, to_right, up, down = first_copies(w)
        to_left.start()
        to_right.start()
        up.start()

        @pl.when(lat > 0)
        def _():
            down.start()

    def pass_corners(w):
        to_left, to_right, _, _ = first_copies(w)
        to_left.wait_recv()
        to_right.wait_recv()
        up, down = corner_copies(w)
        up.start()

        @pl.when(lat > 0)
        def _():
            down.start()

    def finish_halo(w):
        send, recv = hs_send.at[w], hs_recv.at[w]

        def arrived(slot):
            remote(own.at[w, pl.ds(0, cols)], halo.at[w, slot, pl.ds(0, cols)],
                   send.at[3], recv.at[2 + slot], downward).wait_recv()
            remote(colrecv.at[w], halo.at[w, slot, pl.ds(cols, 2 * rows)],
                   send.at[5], recv.at[4 + slot], downward).wait_recv()

        arrived(NORTH)

        @pl.when(lat > 0)
        def _():
            arrived(SOUTH)

    def finish_sends(w):
        to_left, to_right, up, down = first_copies(w)
        up2, down2 = corner_copies(w)
        for copy in (to_left, to_right, up, up2):
            copy.wait_send()

        @pl.when(lat > 0)
        def _():
            down.wait_send()
            down2.wait_send()

    def spread(w, ref, values, order):
        lane = [b * wide for b in order]
        body = pl.ds(0, cells)
        ref[body, lane[1] : lane[1] + ch] = own[w]
        ref[body, lane[0] : lane[0] + ch] = pltpu.roll(values, 1, 0).astype(BF16)
        ref[body, lane[2] : lane[2] + ch] = pltpu.roll(values, cells - 1, 0).astype(BF16)

    def patch(w, ref, order):
        line = iota((SUB, ch), 0)
        margin = colrecv[w].astype(F32)
        for j in range(rows):
            for b, at, spot in ((0, j * cols, 0), (2, (j + 1) * cols - SUB, SUB - 1)):
                lane = order[b] * wide
                here = (slice(at, at + SUB), slice(lane, lane + ch))
                value = margin[j + (rows if b else 0)][None]
                ref[here] = jnp.where(
                    line == spot, value, ref[here].astype(F32)
                ).astype(BF16)

    def spread_halo(w, ref, order):
        shape = (3 * cols, cols + 2 * rows)
        p, s = iota(shape, 0), iota(shape, 1)
        block = jnp.where(p >= cols, 1, 0) + jnp.where(p >= 2 * cols, 1, 0)
        east = p - cols * block + block - 1
        flip = jnp.where(top, 1, 0)
        for slot, at in ((NORTH, cells), (SOUTH, cells + cols)):
            if slot == NORTH:
                e = east + flip * (cols - 1 - 2 * east)
                edge = flip * (rows - 1)
            else:
                e, edge = east, rows - 1
            source = jnp.where(
                e < 0, cols + edge, jnp.where(e >= cols, cols + rows + edge, e))
            got = mm(onehot(s == source), halo[w, slot]).astype(BF16)
            for b in range(3):
                ref[at : at + cols, order[b] * wide : order[b] * wide + ch] = got[
                    b * cols : (b + 1) * cols
                ]

    start_first(0)
    fetch[3].wait()
    k_north[...] = jnp.zeros_like(k_north)
    for c in range(3):
        gap = pl.ds(c * wide + LANE, LANE)
        for ref in (wide_x, wide_g, lag_g):
            ref[:, gap] = jnp.zeros((ref.shape[0], LANE), BF16)
    for r, lo, hi in (
        (0, cells - cols, cells + cols), (1, cells, cells + 2 * cols),
        (2, 0, cols), (2, cells + cols, cells + 2 * cols),
    ):
        lag_g[lo:hi, r * wide : (r + 1) * wide] = jnp.zeros((hi - lo, wide), BF16)
    for r in range(3):
        k_bwd[r] = jnp.zeros_like(k_bwd[r])
        for c in range(3):
            k_fwd[r, c * wide + ch : (c + 1) * wide, :] = jnp.zeros((wide - ch, ch), BF16)
    for r in range(3):
        for c in range(3):
            k_fwd[r, c * wide : c * wide + ch, :] = weights[r, c]
            k_bwd[r, :, c * wide : c * wide + ch] = weights[r, c]

    @pl.when(top)
    def _():
        for c in range(3):
            k_north[:, c * wide : c * wide + ch] = weights[2, 2 - c]

    @pl.when(jnp.logical_not(top))
    def _():
        for c in range(3):
            k_north[:, c * wide : c * wide + ch] = weights[0, c]

    spread(0, wide_x, masked, (0, 1, 2))
    pass_corners(0)
    patch(0, wide_x, (0, 1, 2))
    fetch[4].wait()

    def activate(lo, hi, pre):
        here = keep[lo:hi]
        sig = 0.5 * jnp.tanh(0.5 * pre) + 0.5
        first, last = lo // cols, hi // cols
        shape = (1, last - first, cols, ch)
        out[:, first:last] = (here * pre * sig).astype(BF16).reshape(shape)
        slope = sig * (1.0 + pre * (1.0 - sig))
        upstream = cotangent[:, first:last].reshape(hi - lo, ch).astype(F32)
        grad = (here * upstream * slope).astype(BF16)
        own[1, lo:hi] = grad
        lag_g[lo:hi, wide : wide + ch] = grad
        for r, step in ((0, -cols), (2, cols)):
            a, b = lo + step, hi + step
            if a < 0:
                lag_g[cells + cols : cells + 2 * cols, 0:ch] = grad[:cols]
                grad_in, a = grad[cols:], 0
            elif b > cells:
                lag_g[cells : cells + cols, 2 * wide : 2 * wide + ch] = grad[hi - lo - cols :]
                grad_in, b = grad[: hi - lo - cols], cells
            else:
                grad_in = grad
            if b > a:
                lag_g[a:b, r * wide : r * wide + ch] = grad_in

    for c in range(3):
        x_turned[c, :, 0:cells] = wide_x[0:cells, c * wide : (c + 1) * wide].T
    pre = mm(wide_x[0:cells, :], k_fwd[1])
    low = mm(wide_x[0 : cells - cols, :], k_fwd[0])
    high = mm(wide_x[cols:cells, :], k_fwd[2])
    mid = slice(cols, cells - cols)
    activate(cols, cells - cols, pre[mid] + low[: cells - 2 * cols] + high[cols:])
    finish_halo(0)
    spread_halo(0, wide_x, (0, 1, 2))
    for c in range(3):
        x_turned[c, :, cells:] = wide_x[cells:, c * wide : (c + 1) * wide].T
    low_edge = mm(wide_x[cells + cols :, :], k_fwd[0])
    high_edge = mm(wide_x[cells : cells + cols, :], k_fwd[2])
    activate(0, cols, pre[:cols] + high[:cols] + low_edge)
    activate(cells - cols, cells, pre[cells - cols :] + low[cells - 2 * cols :] + high_edge)
    colsend[1] = mm(pick, own[1]).astype(BF16)
    start_first(1)

    units = ch // SUB
    hl = LANE // 2
    tails = {}

    def add_up(p):
        q = parts[p]
        full = mm(x_turned[p], lag_g[...])
        band = full[:ch]
        slabs = [band[:, r * wide : r * wide + LANE] for r in range(3)]
        rest = [band[:, r * wide + LANE : (r + 1) * wide] for r in range(3)]
        slabs.append(rest[0] + pltpu.roll(rest[1], hl, 1))
        tails[p] = rest[2]
        if p == 1:
            slabs.append(tails[0] + pltpu.roll(tails[1], hl, 1))
        if p == 2:
            slabs.append(tails[2])
        for at, value in enumerate(slabs):
            value = value.reshape(units, SUB, LANE)
            q["wf"][at * units : (at + 1) * units] = value
            q["wb"][at * units : (at + 1) * units] = value.astype(BF16)
        used = len(slabs) * units
        total = q["wf"].shape[0]
        if total > used:
            q["wf"][used:] = jnp.zeros_like(q["wf"][used:])
            q["wb"][used:] = jnp.zeros_like(q["wb"][used:])
        half = total // 2
        q["half"], q["per"] = half, half // npl
        q["chunk"] = q["r3"].shape[1]
        q["pair"] = remote(
            q["wb"].at[pl.ds((1 - core) * half, half)], q["r1"],
            q["s"].at[0, 0], q["q"].at[0, 0], pair)
        q["pair"].start()

    def over_plane(p):
        q = parts[p]
        half = q["half"]
        q["pair"].wait()
        first = q["wf"][pl.ds(core * half, half)] + q["r1"][...].astype(F32)
        q["a1"][...] = first.reshape(q["a1"].shape)
        q["b1"][...] = first.reshape(q["a1"].shape).astype(BF16)
        q["plane"] = []
        for d in range(1, npl):
            index, where = plane_peer(d)
            copy = remote(q["b1"].at[index], q["r2"].at[d - 1],
                          q["s"].at[1, d - 1], q["q"].at[1, d - 1], where)
            copy.start()
            q["plane"].append(copy)

    def over_z(p):
        q = parts[p]
        per, chunk = q["per"], q["chunk"]
        for copy in q["plane"]:
            copy.wait()
        second = q["a1"][plane]
        for d in range(npl - 1):
            second = second + q["r2"][d].astype(F32)
        q["a2"][0:per] = second
        q["b2"][0:per] = second.astype(BF16)
        if nz * chunk > per:
            q["a2"][per:] = jnp.zeros_like(q["a2"][per:])
            q["b2"][per:] = jnp.zeros_like(q["b2"][per:])
        q["z"] = []
        for d in range(1, nz):
            index, where = z_peer(d)
            copy = remote(q["b2"].at[pl.ds(index * chunk, chunk)], q["r3"].at[d - 1],
                          q["s"].at[2, d - 1], q["q"].at[2, d - 1], where)
            copy.start()
            q["z"].append(copy)

    def z_return(p):
        q = parts[p]
        chunk = q["chunk"]
        for copy in q["z"]:
            copy.wait()
        mine = pl.ds(z * chunk, chunk)
        third = q["a2"][mine]
        for d in range(nz - 1):
            third = third + q["r3"][d].astype(F32)
        here = q["ag"].at[core, plane, mine]
        q["ag"][core, plane, mine] = (third * scale).astype(BF16)
        q["sent"] = []
        for d in range(1, nz):
            copy = remote(here, here, q["s"].at[3, d - 1], q["q"].at[3, d - 1], z_peer(d)[1])
            copy.start()
            q["sent"].append(copy)

    def plane_return(p):
        q = parts[p]
        chunk, per = q["chunk"], q["per"]
        for d in range(1, nz):
            source = lax.rem(z + nz - d, nz)
            there = q["ag"].at[core, plane, pl.ds(source * chunk, chunk)]
            remote(there, there, q["s"].at[3, d - 1], q["q"].at[3, d - 1], pair).wait_recv()
        here = q["ag"].at[core, plane, pl.ds(0, per)]
        for d in range(1, npl):
            copy = remote(here, here, q["s"].at[4, d - 1], q["q"].at[4, d - 1], plane_peer(d)[1])
            copy.start()
            q["sent"].append(copy)
        copy = remote(here, here, q["s"].at[5, 0], q["q"].at[5, 0], pair)
        copy.start()
        q["sent"].append(copy)

    def core_return(p):
        q = parts[p]
        for d in range(1, npl):
            source = lax.rem(plane + npl - d, npl)
            there = q["ag"].at[core, source, pl.ds(0, q["per"])]
            remote(there, there, q["s"].at[4, d - 1], q["q"].at[4, d - 1], pair).wait_recv()
            copy = remote(there, there, q["s"].at[5, d], q["q"].at[5, d], pair)
            copy.start()
            q["sent"].append(copy)

    def hand_out(p):
        q = parts[p]
        half, per = q["half"], q["per"]
        for d in range(npl):
            source = lax.rem(plane + npl - d, npl)
            there = q["ag"].at[1 - core, source, pl.ds(0, per)]
            remote(there, there, q["s"].at[5, d], q["q"].at[5, d], pair).wait_recv()

        def slab(at):
            found = []
            for t in range(at * units, (at + 1) * units):
                found.append(q["ag"][t // half, t % half // per, t % per])
            return jnp.concatenate(found, axis=0).astype(F32)

        for r in range(3):
            wgrad[r, p, :, 0:LANE] = slab(r)
        rest = slab(3)
        wgrad[0, p, :, LANE:ch] = rest[:, 0:hl]
        wgrad[1, p, :, LANE:ch] = pltpu.roll(rest, hl, 1)[:, 0:hl]
        if p == 1:
            rest = slab(4)
            wgrad[2, 0, :, LANE:ch] = rest[:, 0:hl]
            wgrad[2, 1, :, LANE:ch] = pltpu.roll(rest, hl, 1)[:, 0:hl]
        if p == 2:
            wgrad[2, 2, :, LANE:ch] = slab(4)[:, 0:hl]

    nt = ((1,), (1,))
    add_up(0)
    add_up(1)
    over_plane(0)
    add_up(2)
    over_plane(1)
    pass_corners(1)
    spread(1, wide_g, own[1].astype(F32), (2, 1, 0))
    over_plane(2)
    patch(1, wide_g, (2, 1, 0))
    back = mm(wide_g[0:cells, :], k_bwd[1], nt)
    over_z(0)
    finish_halo(1)
    spread_halo(1, wide_g, (2, 1, 0))
    over_z(1)
    below = mm(wide_g[0 : cells - cols, :], k_bwd[2], nt)
    below_edge = mm(wide_g[cells + cols :, :], k_bwd[2], nt)
    back = back + jnp.concatenate([below_edge, below], axis=0)
    z_return(0)
    over_z(2)
    z_return(1)
    inner = mm(wide_g[cols:cells, :], k_bwd[0], nt)
    edge = mm(wide_g[cells : cells + cols, :], k_north[...], nt)
    back = back + jnp.concatenate([inner, edge], axis=0)
    sgrad[...] = jnp.where(keep > 0, back, 0.0).astype(BF16).reshape(sgrad.shape)
    plane_return(0)
    z_return(2)
    plane_return(1)
    plane_return(2)
    core_return(0)
    core_return(1)
    hand_out(0)
    core_return(2)
    hand_out(1)
    hand_out(2)

    finish_sends(0)
    finish_sends(1)
    for q in parts:
        for copy in q["sent"]:
            copy.wait_send()


def write_body(out, sgrad, wgrad, out_hbm, sgrad_hbm, wgrad_hbm, save):
    steps = []
    for src, dst in ((out, out_hbm), (sgrad, sgrad_hbm)):
        step = src.shape[1] // 4
        for k in range(4):
            piece = (0, pl.ds(k * step, step))
            steps.append((src.at[piece], dst.at[piece]))
    for r in range(3):
        for k in range(3):
            steps.append((wgrad.at[r, k], wgrad_hbm.at[r, k]))
    saves = [pltpu.make_async_copy(y, w, save.at[i]) for i, (y, w) in enumerate(steps)]
    for copy in saves:
        copy.start()
    for copy in saves:
        copy.wait()


def body(states, cotangent, weights, land_mask, ocean_tiles):
    n_lon, n_lat, n_dp = (lax.axis_size(a) for a in ("lon", "lat", "dp"))
    batch, rows, cols, ch = states.shape
    assert batch == 1 and ch == 192 and n_lon % 2 == 0 and cols & (cols - 1) == 0
    cells = rows * cols
    count = batch * n_dp * rows * n_lat * cols * n_lon
    wide = 2 * LANE
    nz, npl = n_lon // 2, n_lat * n_dp
    groups = 2 * npl
    tile = (SUB, LANE)
    vmem = pltpu.VMEM
    dma = pltpu.SemaphoreType.DMA

    def part_scratch(slabs):
        total = -(-slabs * (ch // SUB) // groups) * groups
        half = total // 2
        per = half // npl
        chunk = -(-per // nz)
        most = max(npl, nz)
        return {
            "wf": vmem((total,) + tile, F32),
            "wb": vmem((total,) + tile, BF16),
            "r1": vmem((half,) + tile, BF16),
            "a1": vmem((npl, per) + tile, F32),
            "b1": vmem((npl, per) + tile, BF16),
            "r2": vmem((npl - 1, per) + tile, BF16),
            "a2": vmem((nz * chunk,) + tile, F32),
            "b2": vmem((nz * chunk,) + tile, BF16),
            "r3": vmem((nz - 1, chunk) + tile, BF16),
            "ag": vmem((2, npl, nz * chunk) + tile, BF16),
            "s": dma((6, most)),
            "q": dma((6, most)),
        }

    scratch = [
        vmem(states.shape, BF16),
        vmem(states.shape, BF16),
        vmem(weights.shape, BF16),
        vmem(land_mask.shape, jnp.int32),
        vmem(ocean_tiles.shape, jnp.int32),
        dma((5,)),
        vmem((2, cells, ch), BF16),
        vmem((2, 2 * rows, ch), BF16),
        vmem((2, 2 * rows, ch), BF16),
        vmem((2, 2, cols + 2 * rows, ch), BF16),
        vmem((cells + 2 * cols, 3 * wide), BF16),
        vmem((cells + 2 * cols, 3 * wide), BF16),
        vmem((cells + 2 * cols, 3 * wide), BF16),
        vmem((3, 3 * wide, ch), BF16),
        vmem((3, ch, 3 * wide), BF16),
        vmem((ch, 3 * wide), BF16),
        vmem((3, wide, cells + 2 * cols), BF16),
        [part_scratch(slabs) for slabs in (4, 5, 5)],
        dma((2, 6)), dma((2, 6)),
    ]
    in_vmem = pl.BlockSpec(memory_space=pltpu.VMEM)
    in_hbm = pl.BlockSpec(memory_space=pltpu.HBM)
    geo = (n_lon, n_lat, n_dp, 1.0 / math.sqrt(count))
    pinned = [
        pltpu.with_memory_space_constraint(v, pltpu.HBM)
        for v in (states, cotangent, weights, land_mask, ocean_tiles)
    ]
    results = pl.pallas_call(
        functools.partial(kernel_body, geo),
        out_shape=(
            vmem(states.shape, BF16),
            vmem(states.shape, BF16),
            vmem(weights.shape, F32),
        ),
        in_specs=[in_hbm] * 5,
        out_specs=(in_vmem,) * 3,
        scratch_shapes=scratch,
        compiler_params=pltpu.CompilerParams(
            collective_id=0, has_side_effects=True, vmem_limit_bytes=40 * 2**20
        ),
        cost_estimate=pl.CostEstimate(
            flops=54 * cells * ch * ch, bytes_accessed=5_000_000, transcendentals=cells * ch
        ),
    )(*pinned)
    return pl.pallas_call(
        write_body,
        out_shape=tuple(jax.ShapeDtypeStruct(v.shape, v.dtype) for v in results),
        in_specs=[in_vmem] * 3,
        out_specs=(in_hbm,) * 3,
        scratch_shapes=[dma((17,))],
        compiler_params=pltpu.CompilerParams(vmem_limit_bytes=2**20),
    )(*results)


def solution(mesh):
    in_specs = (
        P("dp", "lat", "lon", None),
        P("dp", "lat", "lon", None),
        P(),
        P("lat", "lon"),
        P("lat", "lon", None),
    )
    out_specs = (P("dp", "lat", "lon", None), P("dp", "lat", "lon", None), P())
    return jax.shard_map(body, mesh=mesh, in_specs=in_specs, out_specs=out_specs, check_vma=False)
```
